256 devices in a mesh: dp: 64 (over x, y, z_hi, core), tp: 4 (over z_lo).
Axes of the slice: x: 4, y: 4, z: 8 (z_hi: 2, z_lo: 4; z = z_hi * 4 + z_lo), core: 2. Of those that a mesh axis runs over, the one named last changes fastest.
Arguments:
- queries: bfloat16 [384, 128, 576], P('dp', 'tp'), may hold values from -100 to 100
- latent_cache: bfloat16 [384, 320, 576], P('dp'), may hold values from -5 to 5
- lengths: int32 [384], P('dp'), may hold values from 2 to 320, as said below
- slot_row: int32 [384], replicated, may hold values from 0 to 383, each once
- w_uv: bfloat16 [128, 512, 128], P('tp'), may hold values from -0.25 to 0.25
- w_o: bfloat16 [16384, 7168], P('tp', 'dp'), may hold values from -0.046875 to 0.046875
- resid: bfloat16 [384, 7168], P(None, 'dp'), may hold values from -3 to 3
- norm_gain: bfloat16 [7168], replicated, may hold values from 0.099609375 to 1.8984375
- w_gate: bfloat16 [7168, 18432], P('tp', 'dp'), may hold values from -0.0625 to 0.0625
- w_up: bfloat16 [7168, 18432], P('tp', 'dp'), may hold values from -0.0625 to 0.0625
- w_down: bfloat16 [18432, 7168], P('dp', 'tp'), may hold values from -0.046875 to 0.046875
Outputs:
- layer_out: bfloat16 [384, 7168], P('dp', 'tp')
The draws below stay inside these ranges and needn't reach their ends.
Inputs may be any that keep to these rules, and one draw needn't show every extreme that they name: `lengths`: each row's live length; every row has at least positions 0 and 1 live, and some row reaches 320.
All inputs are finite; a program needn't handle non-finite values.
Results may differ from the reference program's by a relative error of at most 0.02.
Values may be sent and summed in bfloat16 or wider, within the bound.
A program may use at most 64 MiB of HBM per device.

```python
import jax
import jax.numpy as jnp
from jax import lax

D = 7168
FF = 18432
H = 128
KL = 512
KR = 64
VD = 128
R = 6
L = 320
ROWS = 384


def shared_cache(key):
    base = jax.random.normal(jax.random.fold_in(key, 11), (ROWS, L, KL + KR), jnp.float32)
    return jnp.clip(base, -5.0, 5.0)


def draw_latent_cache(key, part):
    cache = shared_cache(key)
    return cache.astype(jnp.bfloat16)


def draw_queries(key, part):
    key = jax.random.fold_in(key, 7)
    first = jax.random.fold_in(key, 0)
    values = jnp.clip(jax.random.normal(first, (ROWS, H, KL + KR), jnp.float32), -5.0, 5.0)
    return values.astype(jnp.bfloat16)


def draw_lengths(key, part):
    key = jax.random.fold_in(key, 9)
    first, second, third = jax.random.split(key, 3)
    groups = ROWS // R
    caps = jax.random.randint(first, (groups, 1), L // 8, L + 1)
    counts = jax.random.randint(second, (groups, R), 2, caps + 1).reshape(ROWS)
    chosen = jax.random.randint(third, (), 0, ROWS)
    return counts.at[chosen].set(L).astype(jnp.int32)


def block_scale(stream_key, shape, cuts, least, high):
    loudness, own = 1.0, jax.random.fold_in(stream_key, 6)
    for position, shards_of in cuts:
        draws = jnp.exp(jax.random.uniform(jax.random.fold_in(own, position), (shards_of,), jnp.float32, least / len(cuts), high / len(cuts)))
        loudness = loudness * jnp.repeat(draws, shape[position] // shards_of).reshape([-1 if axis == position else 1 for axis in range(len(shape))])
    return loudness


def gaussian(own_key, dims, width, bound, cuts=(), kind=jnp.bfloat16):
    entries = jax.random.normal(own_key, dims, jnp.float32) * width
    if len(cuts) > 0:
        entries = block_scale(own_key, dims, cuts, -0.22, 0.18) * entries
    return jnp.clip(entries, min=-bound, max=bound).astype(kind)


def setup_inputs(seed: int = 0) -> dict:
    seeds = jax.random.split(jax.random.key(seed), 12)
    return {
        "queries": draw_queries(jax.random.fold_in(seeds[11], 71), 0),
        "latent_cache": draw_latent_cache(jax.random.fold_in(seeds[11], 71), 0),
        "lengths": draw_lengths(jax.random.fold_in(seeds[11], 71), 0),
        "slot_row": jax.random.permutation(seeds[3], ROWS).astype(jnp.int32),
        "w_uv": gaussian(seeds[4], (H, KL, VD), KL ** -0.5, 0.25, ((0, 4),)),
        "w_o": gaussian(seeds[5], (H * VD, D), (H * VD) ** -0.5, 0.046875, ((0, 4), (1, 64))),
        "resid": gaussian(seeds[6], (ROWS, D), 0.5, 3.0, ((1, 64),)),
        "norm_gain": jnp.clip(1.0 + 0.18 * jax.random.normal(seeds[7], (D,), jnp.float32), 0.099609375, 1.8984375).astype(jnp.bfloat16),
        "w_gate": gaussian(seeds[8], (D, FF), D ** -0.5, 0.0625, ((0, 4), (1, 64))),
        "w_up": gaussian(seeds[9], (D, FF), D ** -0.5, 0.0625, ((0, 4), (1, 64))),
        "w_down": gaussian(seeds[10], (FF, D), FF ** -0.5, 0.046875, ((0, 64), (1, 4))),
    }


softmax_scale = 192.0 ** (-0.5)

def attend(args):
    query, cache, count = args
    scores = jnp.einsum('hk,pk->hp', query.astype(jnp.float32), cache.astype(jnp.float32)) * softmax_scale
    live = jnp.arange(L)[None, :] < count
    top = lax.optimization_barrier(jnp.max(jnp.where(live, scores, -1e+30), axis=1, keepdims=True))
    weights = jnp.where(live, jnp.exp(scores - top), 0.0)
    probs = (weights / lax.optimization_barrier(jnp.sum(weights, axis=1, keepdims=True))).astype(jnp.bfloat16)
    latent_out = jnp.einsum('hp,pk->hk', probs.astype(jnp.float32), cache[:, :KL].astype(jnp.float32))
    return latent_out.astype(jnp.bfloat16)

def reference(queries, latent_cache, lengths, slot_row, w_uv, w_o, resid, norm_gain, w_gate, w_up, w_down):
    latent_out = lax.map(attend, (queries, latent_cache, lengths))
    values = jnp.einsum('shk,hkd->shd', latent_out.astype(jnp.float32), w_uv.astype(jnp.float32))
    values = values.astype(jnp.bfloat16).reshape(ROWS, H * VD)
    attention = jnp.dot(values, w_o, preferred_element_type=jnp.float32)
    inverse = jnp.zeros((ROWS,), jnp.int32).at[slot_row].set(jnp.arange(ROWS, dtype=jnp.int32))
    placed = attention[inverse]
    hidden_state = (resid.astype(jnp.float32) + placed).astype(jnp.bfloat16)
    wide = hidden_state.astype(jnp.float32)
    scale_rows = lax.rsqrt(lax.optimization_barrier(jnp.mean(wide * wide, axis=1, keepdims=True)) + 1e-06)
    normed = (wide * scale_rows * norm_gain.astype(jnp.float32)).astype(jnp.bfloat16)
    gate = jnp.dot(normed, w_gate, preferred_element_type=jnp.float32)
    up = jnp.dot(normed, w_up, preferred_element_type=jnp.float32)
    activated = (jax.nn.silu(gate) * up).astype(jnp.bfloat16)
    down = jnp.dot(activated, w_down, preferred_element_type=jnp.float32)
    return (wide + down).astype(jnp.bfloat16)
```

```python
import jax
import jax.numpy as jnp
from jax import lax
from jax.experimental import pallas as pl
from jax.experimental.pallas import tpu as pltpu
from jax.sharding import PartitionSpec as P

MESH = pl.DeviceIdType.MESH
F32 = jnp.float32
BF16 = jnp.bfloat16
SCALE = 192.0 ** (-0.5)
SEMS = 160


def iota(shape, axis):
    return lax.broadcasted_iota(jnp.int32, shape, axis)


def by(value, n):
    return ((value.astype(F32) + 0.5) * (1.0 / n)).astype(jnp.int32)


def dot(a, b):
    return jnp.dot(a, b, preferred_element_type=F32)


def one_hot(hit):
    return jnp.where(hit, 1.0, 0.0).astype(BF16)


def kernel(
    q_hbm, cache_hbm, len_ref, slot_ref, wuv_hbm, wo_hbm, resid_hbm, gain_ref, wg_hbm, wu_hbm, wd_hbm,
    out_ref,
    q_v, cache_v, wuv_v, wo_v, resid_v, wg_v, wu_v, wd_v,
    lat_s, msg_s, abuf, perm_s, z_s, wo_s, r_s, p_s, b_rx,
    cbuf, hid_s, x_s, w_s, ss_s, ss_rx, gu_s, d_rx, act_s,
    pta_s, ptb_s, t_s, hm_s, hm_rx, hid_out,
    e1_s, e1_rx, e2_s, e2_rx, u_s, e3_s, e3_rx,
    sems,
):
    dp, t = lax.axis_index("dp"), lax.axis_index("tp")
    c = lax.rem(dp, 2)
    zh = lax.rem(dp // 2, 2)
    y = lax.rem(dp // 4, 4)
    x = dp // 16
    place = dp // 2
    sib = 1 - c
    other = 1 - zh

    def dev(x_, y_, zh_, c_, t_):
        return (((x_ * 4 + y_) * 2 + zh_) * 2 + c_, t_)

    def turn(v, k):
        return lax.rem(v + k + 4, 4)

    used = [0]

    def sem():
        used[0] += 1
        return sems.at[used[0] - 1]

    sends = []

    def remote(src, dst, ss, rs, to):
        return pltpu.make_async_remote_copy(
            src_ref=src, dst_ref=dst, send_sem=ss, recv_sem=rs, device_id=to, device_id_type=MESH
        )

    def send(src, dst, to, landing):
        ss, rs = sem(), sem()
        cp = remote(src, dst, ss, rs, to)
        cp.start()
        sends.append(cp)
        return remote(src, landing, ss, rs, to)

    def load(src, dst):
        cp = pltpu.make_async_copy(src, dst, sem())
        cp.start()
        return cp

    sib_dev = dev(x, y, zh, sib, t)
    zh_dev = dev(x, y, other, c, t)
    x_dev = [dev(turn(x, k), y, zh, c, t) for k in range(4)]
    y_dev = [dev(x, turn(y, k), zh, c, t) for k in range(4)]
    t_dev = [(dp, turn(t, k)) for k in range(4)]

    q_in = load(q_hbm, q_v)
    cache_in = [load(cache_hbm.at[r], cache_v.at[r]) for r in range(6)]
    wuv_in = [load(wuv_hbm.at[pl.ds(16 * i, 16)], wuv_v.at[pl.ds(16 * i, 16)]) for i in range(2)]
    later = [
        load(resid_hbm, resid_v.at[c]),
        load(wo_hbm, wo_v.at[c]),
        load(wg_hbm, wg_v.at[c]),
        load(wu_hbm, wu_v.at[c]),
        load(wd_hbm.at[pl.ds(0, 256)], wd_v.at[pl.ds(pl.multiple_of(256 * c, 256), 256)]),
        load(wd_hbm.at[pl.ds(256, 32)], wd_v.at[pl.ds(pl.multiple_of(512 + 32 * c, 32), 32)]),
    ]
    barrier = pltpu.get_barrier_semaphore()
    for d in [sib_dev, zh_dev] + x_dev[1:] + y_dev[1:] + t_dev[1:]:
        pl.semaphore_signal(barrier, inc=1, device_id=d, device_id_type=MESH)
    for k in range(4):

        @pl.when(jnp.logical_or(x != t, k != t))
        def _():
            pl.semaphore_signal(barrier, inc=1, device_id=dev(t, y, zh, c, k), device_id_type=MESH)

    for j in range(4):
        lat_s[j, pl.ds(6, 32, 8), :] = jnp.zeros((32, 128), F32)
        lat_s[j, pl.ds(7, 32, 8), :] = jnp.zeros((32, 128), F32)
    q_in.wait()
    for r in range(6):
        cache_in[r].wait()
        keys = cache_v[r]
        scores = (
            lax.dot_general(q_v[r], keys, (((1,), (1,)), ((), ())), preferred_element_type=F32) * SCALE
        )
        live = iota((32, 320), 1) < len_ref[r]
        top = jnp.max(jnp.where(live, scores, -1e30), axis=1, keepdims=True)
        weights = jnp.where(live, jnp.exp(scores - top), 0.0)
        probs = (weights / jnp.sum(weights, axis=1, keepdims=True)).astype(BF16)
        latent = dot(probs, keys[:, :512])
        for j in range(4):
            lat_s[j, pl.ds(r, 32, 8), :] = latent[:, 128 * j : 128 * j + 128]
    for half in range(2):
        wuv_in[half].wait()
        for low in range(8):
            for high in range(2):
                h = half * 16 + low * 2 + high
                latent = [lat_s[j, 8 * h : 8 * h + 8, :].astype(BF16) for j in range(4)]
                value = dot(jnp.concatenate(latent, axis=1), wuv_v[h])
                msg_s[half, 6 * low : 6 * low + 8, 128 * high : 128 * high + 128] = value
        abuf[half, x, y, zh] = msg_s[half, 0:48, :].astype(BF16)

    pl.semaphore_wait(barrier, 15 - jnp.where(x == t, 1, 0))

    def across(buf):
        return send(buf.at[:, x, y, zh], buf.at[:, x, y, zh], zh_dev, buf.at[:, x, y, other])

    def first(buf):
        out = []
        for k in range(1, 4):
            out.append(send(buf.at[0, x, y], buf.at[0, x, y], x_dev[k], buf.at[0, turn(x, -k), y]))
            out.append(send(buf.at[1, x, y], buf.at[1, x, y], y_dev[k], buf.at[1, x, turn(y, -k)]))
        return out

    def second(buf):
        out = []
        for k in range(1, 4):
            out.append(send(buf.at[0, :, y], buf.at[0, :, y], y_dev[k], buf.at[0, :, turn(y, -k)]))
            out.append(send(buf.at[1, x], buf.at[1, x], x_dev[k], buf.at[1, turn(x, -k)]))
        return out

    def arrive(copies):
        for cp in copies:
            cp.wait_recv()

    step = across(abuf)
    for cp in later:
        cp.wait()
    theirs = [
        send(resid_v.at[c], resid_v.at[c], sib_dev, resid_v.at[sib]),
        send(wo_v.at[c], wo_v.at[c], sib_dev, wo_v.at[sib]),
        send(wg_v.at[c], wg_v.at[c], sib_dev, wg_v.at[sib]),
        send(wu_v.at[c], wu_v.at[c], sib_dev, wu_v.at[sib]),
    ]
    for at, n in ((0, 256), (512, 32)):
        mine = wd_v.at[pl.ds(pl.multiple_of(at + n * c, n), n)]
        yours = wd_v.at[pl.ds(pl.multiple_of(at + n * sib, n), n)]
        theirs.append(send(mine, mine, sib_dev, yours))

    row, col = iota((384, 384), 0), iota((384, 384), 1)
    low = by(row, 48)
    within = row - 48 * low
    source = by(within, 6)
    perm_s[...] = one_hot(col == source * 48 + low * 6 + (within - 6 * source))
    slots = jnp.broadcast_to(slot_ref[...], (384, 384))
    half_of = jnp.where(col >= 192, 1, 0)
    rho = col - 192 * half_of
    slot_of = 2 * rho - (rho - 6 * by(rho, 6)) + 6 * half_of
    order = one_hot(row == slot_of)
    rho = iota((384, 192), 1)
    order_c = one_hot(iota((384, 192), 0) == 2 * rho - (rho - 6 * by(rho, 6)) + 6 * c)
    line = iota((256, 384), 0)
    inner = line % 8
    for ref, chip in (
        (pta_s, line // 8),
        (ptb_s, ((line // 16) % 4 * 4 + line // 64) * 2 + (line // 8) % 2),
    ):
        want = jnp.where(inner < 6, (chip * 2 + c) * 6 + inner, -1)
        ref[...] = dot(one_hot(slots[:256] == want), order).astype(BF16)
    line = iota((16, 384), 0)
    want = jnp.where(line % 8 < 6, (place * 2 + line // 8) * 6 + line % 8, -1)
    t_s[...] = dot(one_hot(slots[:16] == want), order_c).astype(BF16)
    moved = dot(one_hot(slots == row), order_c).astype(BF16)

    step.wait_recv()
    step = first(abuf)
    for cp in theirs:
        cp.wait_recv()
    r_s[...] = jnp.zeros((192, 256), F32)
    for k in range(2):
        r_s[:, 128 * k : 128 * k + 112] = lax.dot_general(
            moved, resid_v[k], (((0,), (0,)), ((), ())), preferred_element_type=F32
        )
    wo_s[...] = jnp.zeros((4096, 256), BF16)
    for k in range(2):
        wo_s[:, 128 * k : 128 * k + 112] = wo_v[k]
    arrive(step)
    step = second(abuf)
    w_s[...] = jnp.zeros((2048, 1152), BF16)

    def spread(j, _):
        src = pl.ds(pl.multiple_of(j * 112, 16), 112)
        dst = pl.ds(pl.multiple_of(j * 128, 128), 112)
        w_s[dst, 0:256] = wg_v[0, src, 0:256]
        w_s[dst, 256:512] = wg_v[1, src, 0:256]
        w_s[dst, 512:768] = wu_v[0, src, 0:256]
        w_s[dst, 768:1024] = wu_v[1, src, 0:256]
        for k, (ref, which) in enumerate(((wg_v, 0), (wg_v, 1), (wu_v, 0), (wu_v, 1))):
            w_s[dst, 1024 + 32 * k : 1056 + 32 * k] = ref[which, src, 256:288]
        return 0

    lax.fori_loop(0, 16, spread, 0)
    wd_v[576:640, :] = jnp.zeros((64, 1792), BF16)
    arrive(step)

    for half in range(2):
        for k in range(4):
            packed = abuf[half, k].reshape(384, 256)
            placed = dot(perm_s[...], packed).astype(BF16)
            for low in range(8):
                at = half * 2048 + low * 256
                z_s[48 * k : 48 * k + 48, at : at + 256] = placed[48 * low : 48 * low + 48]
    partial = dot(z_s[...], wo_s[...]) + jnp.where(t == 0, r_s[...], 0.0)
    p_s[...] = partial.astype(BF16).reshape(4, 48, 256)
    b_send, b_recv = [sem() for _ in range(4)], used[0]
    used[0] += 4
    for k in range(4):
        own = jnp.logical_and(x == t, k == x)
        cp = remote(p_s.at[k], b_rx.at[t], b_send[k], sems.at[b_recv + t], dev(k, y, zh, c, x))

        @pl.when(jnp.logical_not(own))
        def _():
            cp.start()

        @pl.when(own)
        def _():
            pltpu.make_async_copy(p_s.at[k], b_rx.at[t], sems.at[b_recv + t]).start()

    for k in range(4):
        pltpu.make_async_copy(p_s.at[k], b_rx.at[k], sems.at[b_recv + k]).wait()
    hidden = jnp.sum(b_rx[...].astype(F32), axis=0).astype(BF16)
    for half in range(2):
        cbuf[half, x, y, zh] = hidden[:, 128 * half : 128 * half + 128]

    across(cbuf).wait_recv()
    arrive(first(cbuf))
    arrive(second(cbuf))
    gain = gain_ref[pl.ds(pl.multiple_of(16 * t, 16), 16), :].astype(F32)
    for k in range(4):
        squares = jnp.zeros((48, 128), F32)
        for j in range(16):
            block = cbuf[j % 2, k, j // 4, (j // 2) % 2]
            hid_s[48 * k : 48 * k + 48, 128 * j : 128 * j + 128] = block
            block = block.astype(F32)
            squares += block * block
            x_s[48 * k : 48 * k + 48, 128 * j : 128 * j + 128] = (block * gain[j : j + 1]).astype(BF16)
        ss_s[k] = jnp.broadcast_to(jnp.sum(squares, axis=1, keepdims=True), (48, 128))
    step = [
        send(ss_s.at[turn(t, k)], ss_rx.at[k - 1], t_dev[k], ss_rx.at[k - 1]) for k in range(1, 4)
    ]

    gu_s[...] = dot(x_s[...], w_s[...]).astype(BF16).reshape(4, 48, 1152)
    step += [
        send(gu_s.at[turn(t, k)], d_rx.at[k - 1], t_dev[k], d_rx.at[k - 1]) for k in range(1, 4)
    ]
    mine = dot(t_s[...], hid_s[...])
    hm_s[...] = mine.reshape(2, 8, 2048)
    hm_in = send(hm_s.at[sib], hm_rx, sib_dev, hm_rx)
    arrive(step)
    total = gu_s[t].astype(F32)
    squares = ss_s[t]
    for k in range(3):
        total += d_rx[k].astype(F32)
        squares += ss_rx[k]
    total *= lax.rsqrt(squares[:, 0:1] * (1.0 / 7168) + 1e-06)

    def silu(v):
        return v * jax.nn.sigmoid(v)

    rest = total[:, 1024:1152]
    tail = silu(rest) * pltpu.roll(rest, 64, 1)
    act_s[c, t, :, 0:512] = (silu(total[:, 0:512]) * total[:, 512:1024]).astype(BF16)
    act_s[c, t, :, 512:640] = jnp.where(iota((48, 128), 1) < 64, tail, 0.0).astype(BF16)
    step = [
        send(act_s.at[c, t], act_s.at[c, t], t_dev[k], act_s.at[c, turn(t, -k)]) for k in range(1, 4)
    ]
    pairs = [send(act_s.at[c, t], act_s.at[c, t], sib_dev, act_s.at[sib, t])]
    hm_in.wait_recv()
    state = hm_s[c] + hm_rx[...]
    for j in range(16):
        hid_out[:, 112 * j : 112 * j + 112] = state[:, 128 * j : 128 * j + 112]
    for k in range(1, 4):
        step[k - 1].wait_recv()
        at = turn(t, -k)
        pairs.append(send(act_s.at[c, at], act_s.at[c, at], sib_dev, act_s.at[sib, at]))
    arrive(pairs)

    everyone = act_s[...].reshape(384, 640)
    for half, ref in ((0, pta_s), (1, ptb_s)):
        rows = dot(ref[...], everyone).astype(BF16)
        down = dot(rows, wd_v[:, 896 * half : 896 * half + 896])
        e1_s[half] = down.astype(BF16).reshape(4, 64, 896)
    spots = (x, y)
    rings = (x_dev, y_dev)
    step = []
    for half in range(2):
        for k in range(1, 4):
            step.append(
                send(
                    e1_s.at[half, turn(spots[half], k)], e1_rx.at[half, k - 1], rings[half][k],
                    e1_rx.at[half, k - 1],
                )
            )
    arrive(step)
    for half in range(2):
        total = e1_s[half, spots[half]].astype(F32)
        for k in range(3):
            total += e1_rx[half, k].astype(F32)
        e2_s[half] = total.astype(BF16).reshape(4, 16, 896)
    step = []
    for half in range(2):
        for k in range(1, 4):
            step.append(
                send(
                    e2_s.at[half, turn(spots[1 - half], k)], e2_rx.at[half, k - 1], rings[1 - half][k],
                    e2_rx.at[half, k - 1],
                )
            )
    arrive(step)
    for half in range(2):
        total = e2_s[half, spots[1 - half]].astype(F32)
        for k in range(3):
            total += e2_rx[half, k].astype(F32)
        u_s[half] = total.reshape(2, 8, 896)
    e3_s[...] = jnp.concatenate([u_s[0, other], u_s[1, other]], axis=0).astype(BF16)
    send(e3_s, e3_rx, zh_dev, e3_rx).wait_recv()
    last = e3_rx[...].astype(F32)
    for half in range(2):
        at = 896 * half
        total = u_s[half, zh] + last[8 * half : 8 * half + 8] + hid_out[:, at : at + 896]
        out_ref[:, at : at + 896] = total[0:6].astype(BF16)

    for k in range(4):

        @pl.when(jnp.logical_not(jnp.logical_and(x == t, k == x)))
        def _():
            remote(p_s.at[k], b_rx.at[t], b_send[k], sems.at[b_recv + t], dev(k, y, zh, c, x)).wait_send()

    for cp in sends:
        cp.wait_send()


def on_device(
    queries, latent_cache, lengths, slot_row, w_uv, w_o, resid, norm_gain, w_gate, w_up, w_down
):
    slots = slot_row.reshape(1, 384)
    gain = jnp.pad(norm_gain.reshape(64, 112), ((0, 0), (0, 16)))
    hbm = pl.BlockSpec(memory_space=pl.ANY)
    vmem = pl.BlockSpec(memory_space=pltpu.VMEM)
    smem = pl.BlockSpec(memory_space=pltpu.SMEM)
    scratch = [
        ((6, 32, 576), BF16),
        ((6, 320, 576), BF16),
        ((32, 512, 128), BF16),
        ((2, 4096, 112), BF16),
        ((2, 384, 112), BF16),
        ((2, 1792, 288), BF16),
        ((2, 1792, 288), BF16),
        ((640, 1792), BF16),
        ((4, 256, 128), F32),
        ((2, 56, 256), F32),
        ((2, 4, 4, 2, 48, 256), BF16),
        ((384, 384), BF16),
        ((192, 4096), BF16),
        ((4096, 256), BF16),
        ((192, 256), F32),
        ((4, 48, 256), BF16),
        ((4, 48, 256), BF16),
        ((2, 4, 4, 2, 48, 128), BF16),
        ((192, 2048), BF16),
        ((192, 2048), BF16),
        ((2048, 1152), BF16),
        ((4, 48, 128), F32),
        ((3, 48, 128), F32),
        ((4, 48, 1152), BF16),
        ((3, 48, 1152), BF16),
        ((2, 4, 48, 640), BF16),
        ((256, 384), BF16),
        ((256, 384), BF16),
        ((16, 192), BF16),
        ((2, 8, 2048), F32),
        ((8, 2048), F32),
        ((8, 1792), F32),
        ((2, 4, 64, 896), BF16),
        ((2, 3, 64, 896), BF16),
        ((2, 4, 16, 896), BF16),
        ((2, 3, 16, 896), BF16),
        ((2, 2, 8, 896), F32),
        ((16, 896), BF16),
        ((16, 896), BF16),
    ]
    return pl.pallas_call(
        kernel,
        out_shape=jax.ShapeDtypeStruct((6, 1792), BF16),
        in_specs=[hbm, hbm, smem, vmem, hbm, hbm, hbm, vmem, hbm, hbm, hbm],
        out_specs=vmem,
        scratch_shapes=[pltpu.VMEM(s, d) for s, d in scratch] + [pltpu.SemaphoreType.DMA((SEMS,))],
        compiler_params=pltpu.CompilerParams(
            collective_id=0, has_side_effects=True, vmem_limit_bytes=58 * 1024 * 1024
        ),
        name="layer",
    )(queries, latent_cache, lengths, slots, w_uv, w_o, resid, gain, w_gate, w_up, w_down)


def solution(mesh):
    placed = (
        P("dp", "tp", None),
        P("dp", None, None),
        P("dp"),
        P(),
        P("tp", None, None),
        P("tp", "dp"),
        P(None, "dp"),
        P(),
        P("tp", "dp"),
        P("tp", "dp"),
        P("dp", "tp"),
    )
    return jax.shard_map(
        on_device, mesh=mesh, in_specs=placed, out_specs=P("dp", "tp"), check_vma=False
    )
```

```python
import jax
import jax.numpy as jnp
from jax import lax
from jax.experimental import pallas as pl
from jax.experimental.pallas import tpu as pltpu
from jax.sharding import PartitionSpec as P

MESH = pl.DeviceIdType.MESH
F32 = jnp.float32
BF16 = jnp.bfloat16
SCALE = 192.0 ** (-0.5)
SEMS = 400


def iota(shape, axis):
    return lax.broadcasted_iota(jnp.int32, shape, axis)


def by(value, n):
    return ((value.astype(F32) + 0.5) * (1.0 / n)).astype(jnp.int32)


def dot(a, b):
    return jnp.dot(a, b, preferred_element_type=F32)


def dot_t(a, b):
    return lax.dot_general(a, b, (((1,), (1,)), ((), ())), preferred_element_type=F32)


def one_hot(hit):
    return jnp.where(hit, 1.0, 0.0).astype(BF16)


def kernel(
    q_hbm, cache_hbm, len_hbm, slot_hbm, wuv_hbm, wo_hbm, resid_hbm, gain_hbm, wg_hbm, wu_hbm, wd_hbm,
    out_ref,
    len_ref, slot_ref, gain_ref, gain_s,
    q_v, cache_v, wuv_v, resid_v, wg_v, wu_v, wd_v,
    lat_s, msg_s, abuf, perm_s, z_s, wo_s, slot_s, pt_s, r_s, p_s, b_rx,
    cbuf, hid_s, x_s, w_s, sq_s, ss_s, ss_rx, gu_s, d_rx, act_s,
    turn_s, pad_s, t_s, hid_out,
    e1_s, e1_rx, sum_s, e2_s, e2_rx, u_s, e3_s, e3_rx,
    sems,
):
    dp, t = lax.axis_index("dp"), lax.axis_index("tp")
    c = lax.rem(dp, 2)
    zh = lax.rem(dp // 2, 2)
    y = lax.rem(dp // 4, 4)
    x = dp // 16
    place = dp // 2
    sib = 1 - c
    other = 1 - zh

    def dev(x_, y_, zh_, c_, t_):
        return (((x_ * 4 + y_) * 2 + zh_) * 2 + c_, t_)

    def turn(v, k):
        return lax.rem(v + k + 4, 4)

    used = [0]

    def sem():
        used[0] += 1
        return sems.at[used[0] - 1]

    sends, tails = [], []

    def finish():
        for tail in tails:
            tail()
        for cp in sends:
            cp.wait_send()

    def remote(src, dst, ss, rs, to):
        return pltpu.make_async_remote_copy(
            src_ref=src, dst_ref=dst, send_sem=ss, recv_sem=rs, device_id=to, device_id_type=MESH
        )

    def send(src, dst, to, landing):
        ss, rs = sem(), sem()
        cp = remote(src, dst, ss, rs, to)
        cp.start()
        sends.append(cp)
        return remote(src, landing, ss, rs, to)

    def load(src, dst):
        cp = pltpu.make_async_copy(src, dst, sem())
        cp.start()
        return cp

    sib_dev = dev(x, y, zh, sib, t)
    zh_dev = dev(x, y, other, c, t)
    x_dev = [dev(turn(x, k), y, zh, c, t) for k in range(4)]
    y_dev = [dev(x, turn(y, k), zh, c, t) for k in range(4)]
    t_dev = [(dp, turn(t, k)) for k in range(4)]

    len_in = load(len_hbm, len_ref)
    q_in = load(q_hbm, q_v)
    cache_in = [load(cache_hbm.at[r], cache_v.at[r]) for r in range(6)]
    wuv_in = [load(wuv_hbm.at[pl.ds(16 * i, 16)], wuv_v.at[pl.ds(16 * i, 16)]) for i in range(2)]
    later = [
        load(slot_hbm, slot_ref),
        load(gain_hbm, gain_ref),
        load(resid_hbm, resid_v.at[c]),
        load(wo_hbm, wo_s.at[pl.ds(pl.multiple_of(128 * c, 128), 112)]),
        load(wg_hbm, wg_v.at[c]),
        load(wu_hbm, wu_v.at[c]),
        load(wd_hbm.at[pl.ds(0, 256)], wd_v.at[pl.ds(pl.multiple_of(256 * c, 256), 256)]),
        load(wd_hbm.at[pl.ds(256, 32)], wd_v.at[pl.ds(pl.multiple_of(512 + 32 * c, 32), 32)]),
    ]
    barrier = pltpu.get_barrier_semaphore()
    for d in [sib_dev, zh_dev] + x_dev[1:] + y_dev[1:] + t_dev[1:]:
        pl.semaphore_signal(barrier, inc=1, device_id=d, device_id_type=MESH)
    for k in range(8):

        @pl.when(jnp.logical_or(x != t, zh * 4 + t != k))
        def _():
            pl.semaphore_signal(
                barrier, inc=1, device_id=dev(t, y, k // 4, c, k % 4), device_id_type=MESH
            )

    for j in range(4):
        lat_s[j, pl.ds(6, 32, 8), :] = jnp.zeros((32, 128), F32)
        lat_s[j, pl.ds(7, 32, 8), :] = jnp.zeros((32, 128), F32)
    len_in.wait()
    q_in.wait()
    for r in range(6):
        cache_in[r].wait()
        keys = cache_v[r]
        scores = dot_t(q_v[r], keys) * SCALE
        live = iota((32, 320), 1) < len_ref[r]
        top = jnp.max(jnp.where(live, scores, -1e30), axis=1, keepdims=True)
        weights = jnp.where(live, jnp.exp(scores - top), 0.0)
        probs = (weights / jnp.sum(weights, axis=1, keepdims=True)).astype(BF16)
        latent = dot(probs, keys[:, :512])
        for j in range(4):
            lat_s[j, pl.ds(r, 32, 8), :] = latent[:, 128 * j : 128 * j + 128]
    for half in range(2):
        wuv_in[half].wait()
        for low in range(8):
            for high in range(2):
                h = half * 16 + low * 2 + high
                latent = [lat_s[j, 8 * h : 8 * h + 8, :].astype(BF16) for j in range(4)]
                value = dot(jnp.concatenate(latent, axis=1), wuv_v[h])
                msg_s[half, 6 * low : 6 * low + 8, 128 * high : 128 * high + 128] = value
        abuf[half, x, y, zh] = msg_s[half, 0:48, :].astype(BF16)

    pl.semaphore_wait(barrier, 19 - jnp.where(x == t, 1, 0))

    def arrive(copies):
        for cp in copies:
            cp.wait_recv()

    def first(block):
        out = []
        for k in range(1, 4):
            out.append(send(block(0, x, y), block(0, x, y), x_dev[k], block(0, turn(x, -k), y)))
            out.append(send(block(1, x, y), block(1, x, y), y_dev[k], block(1, x, turn(y, -k))))
        return out

    def second(block):
        out = []
        every = slice(None)
        for k in range(1, 4):
            out.append(send(block(0, every, y), block(0, every, y), y_dev[k], block(0, every, turn(y, -k))))
            out.append(send(block(1, x, every), block(1, x, every), x_dev[k], block(1, turn(x, -k), every)))
        return out

    def near(half, x_, y_):
        return abuf.at[half, x_, y_, zh]

    def far(half, x_, y_):
        return abuf.at[half, x_, y_, other]

    near_in = first(near)
    far_in = send(abuf.at[:, x, y, zh], abuf.at[:, x, y, zh], zh_dev, abuf.at[:, x, y, other])
    for cp in later:
        cp.wait()
    theirs = [
        send(resid_v.at[c], resid_v.at[c], sib_dev, resid_v.at[sib]),
        send(wg_v.at[c], wg_v.at[c], sib_dev, wg_v.at[sib]),
        send(wu_v.at[c], wu_v.at[c], sib_dev, wu_v.at[sib]),
    ]
    for ref, at, step_, n in ((wo_s, 0, 128, 112), (wd_v, 0, 256, 256), (wd_v, 512, 32, 32)):
        ours = ref.at[pl.ds(pl.multiple_of(at + step_ * c, step_), n)]
        other_half = ref.at[pl.ds(pl.multiple_of(at + step_ * sib, step_), n)]
        theirs.append(send(ours, ours, sib_dev, other_half))
    arrive(near_in)
    near_in = second(near)

    row, col = iota((384, 384), 0), iota((384, 384), 1)
    low = by(row, 48)
    within = row - 48 * low
    source = by(within, 6)
    perm_s[...] = one_hot(col == source * 48 + low * 6 + (within - 6 * source))
    far_in.wait_recv()
    far_in = first(far)

    half_of = jnp.where(col >= 192, 1, 0)
    rho = col - 192 * half_of
    slot_of = 2 * rho - (rho - 6 * by(rho, 6)) + 6 * half_of
    order = one_hot(row == slot_of)
    line = iota((192, 384), 0)
    want = ((line % 64) // 2 * 2 + c) * 6 + line // 64 * 2 + line % 2
    slots = jnp.broadcast_to(slot_ref[...][None, :], (192, 384))
    pt_s[...] = dot(one_hot(slots == want), order).astype(BF16)
    rows_here = one_hot(iota((192, 384), 1) == want)
    arrive(far_in)
    far_in = second(far)

    arrive(theirs)
    r_s[...] = jnp.zeros((192, 256), F32)
    for k in range(2):
        r_s[:, 128 * k : 128 * k + 112] = dot_t(rows_here, resid_v[k])
        wo_s[128 * k + 112 : 128 * k + 128, :] = jnp.zeros((16, 4096), BF16)
    gain_s[...] = jnp.zeros((64, 128), F32)
    gains = gain_ref[...].astype(F32)[None, :]
    for j in range(64):
        gain_s[j : j + 1, 0:112] = gains[:, 112 * j : 112 * j + 112]
    line, row = iota((64, 64), 0), iota((64, 64), 1)
    turn_s[...] = one_hot(row == line // 4 % 4 * 16 + line // 16 * 4 + line % 4)
    line, row = iota((64, 48), 0), iota((64, 48), 1)
    pad_s[...] = one_hot(
        jnp.logical_and(line % 8 < 6, row == line % 8 // 2 * 16 + line // 8 * 2 + line % 2)
    )
    line, row = iota((8, 48), 0), iota((8, 48), 1)
    t_s[...] = one_hot(jnp.logical_and(line < 6, row == line // 2 * 16 + (y * 2 + zh) * 2 + line % 2))
    wd_v[576:640, :] = jnp.zeros((64, 1792), BF16)
    w_s[...] = jnp.zeros((1152, 2048), BF16)

    def spread(src, dst):
        for j in range(16):
            dst[:, 128 * j : 128 * j + 112] = src[:, 112 * j : 112 * j + 112]

    for k, ref in enumerate((wg_v, wu_v)):
        for half in range(2):
            at = 512 * k + 256 * half

            def piece(i, _):
                rows = pl.ds(pl.multiple_of(32 * i, 32), 32)
                into = pl.ds(pl.multiple_of(at + 32 * i, 32), 32)
                spread(ref.at[half, rows], w_s.at[into])
                return 0

            lax.fori_loop(0, 8, piece, 0)
            at = 1024 + 64 * k + 32 * half
            spread(ref.at[half, 256:288], w_s.at[at : at + 32])
    arrive(near_in)
    arrive(far_in)

    for half in range(2):
        for k in range(4):
            packed = abuf[half, k].reshape(384, 256)
            placed = dot(perm_s[...], packed).astype(BF16)
            for low in range(8):
                at = half * 2048 + low * 256
                z_s[48 * k : 48 * k + 48, at : at + 256] = placed[48 * low : 48 * low + 48]
    slot_s[c] = dot_t(z_s[...], wo_s[...]).astype(BF16)
    send(slot_s.at[c], slot_s.at[c], sib_dev, slot_s.at[sib]).wait_recv()
    partial = dot(pt_s[...], slot_s[...].reshape(384, 256)) + jnp.where(t == 0, r_s[...], 0.0)
    p_s[...] = partial.astype(BF16).reshape(3, 4, 16, 256)

    b_at = used[0]
    used[0] += 48
    for i in range(3):
        for k in range(4):
            for z_ in range(2):
                own = jnp.logical_and(jnp.logical_and(x == t, k == x), zh == z_)
                arrived = sems.at[b_at + 24 + 8 * i + 4 * zh + t]
                cp = remote(
                    p_s.at[i, k], b_rx.at[i, zh, t], sems.at[b_at + 8 * i + 2 * k + z_], arrived,
                    dev(k, y, z_, c, x),
                )

                @pl.when(jnp.logical_not(own))
                def _():
                    cp.start()

                @pl.when(own)
                def _():
                    pltpu.make_async_copy(p_s.at[i, k], b_rx.at[i, zh, t], arrived).start()

                def sent(cp=cp, own=own):
                    @pl.when(jnp.logical_not(own))
                    def _():
                        cp.wait_send()

                tails.append(sent)

    def blocks(i):
        def block(half, x_, y_):
            return cbuf.at[i, half, x_, y_]

        return block

    step = []
    for i in range(3):
        for z_ in range(2):
            for k in range(4):
                pltpu.make_async_copy(
                    p_s.at[i, k], b_rx.at[i, z_, k], sems.at[b_at + 24 + 8 * i + 4 * z_ + k]
                ).wait()
            hidden = jnp.sum(b_rx[i, z_].astype(F32), axis=0).astype(BF16)
            for half in range(2):
                cbuf[i, half, x, y, z_] = hidden[:, 128 * half : 128 * half + 128]
        step.append(first(blocks(i)))
    for i in range(3):
        arrive(step[i])
        step[i] = second(blocks(i))

    gain = gain_s[pl.ds(pl.multiple_of(16 * t, 16), 16), :]

    def silu(v):
        return v * jax.nn.sigmoid(v)

    def gate_up(i):
        arrive(step[i])
        for k in range(4):
            squares = jnp.zeros((16, 128), F32)
            for j in range(16):
                block = cbuf[i, j % 2, k, j // 4, (j // 2) % 2].astype(F32)
                squares += block * block
                x_s[i, 16 * k : 16 * k + 16, 128 * j : 128 * j + 128] = (block * gain[j : j + 1]).astype(BF16)
            sq_s[16 * k : 16 * k + 16] = squares
        ss_s[i] = lax.dot_general(
            jnp.ones((8, 128), F32), sq_s[...], (((1,), (1,)), ((), ())),
            precision=lax.Precision.HIGHEST, preferred_element_type=F32,
        )
        out = [send(ss_s.at[i], ss_rx.at[i, k - 1], t_dev[k], ss_rx.at[i, k - 1]) for k in range(1, 4)]
        gu_s[i] = dot_t(x_s[i], w_s[...]).astype(BF16).reshape(4, 16, 1152)
        for k in range(1, 4):
            out.append(send(gu_s.at[i, turn(t, k)], d_rx.at[i, k - 1], t_dev[k], d_rx.at[i, k - 1]))
        return out

    def activate(i, copies):
        arrive(copies)
        total = gu_s[i, t].astype(F32)
        squares = ss_s[i]
        for k in range(3):
            total += d_rx[i, k].astype(F32)
            squares += ss_rx[i, k]
        here = iota((16, 64), 1) == 16 * t + iota((16, 64), 0)
        squares = jnp.sum(jnp.where(here, squares[0:1], 0.0), axis=1, keepdims=True)
        total *= lax.rsqrt(squares * (1.0 / 7168) + 1e-06)
        rest = total[:, 1024:1152]
        tail = silu(rest) * pltpu.roll(rest, 64, 1)
        act_s[i, t, :, 0:512] = (silu(total[:, 0:512]) * total[:, 512:1024]).astype(BF16)
        act_s[i, t, :, 512:640] = jnp.where(iota((16, 128), 1) < 64, tail, 0.0).astype(BF16)
        return [
            send(act_s.at[i, t], act_s.at[i, t], t_dev[k], act_s.at[i, turn(t, -k)]) for k in range(1, 4)
        ]

    spots = (x, y)
    rings = (x_dev, y_dev)

    def down(i, copies):
        arrive(copies)
        rows = act_s[i].reshape(64, 640)
        out = []
        for half in range(2):
            if half == 1:
                rows = dot(turn_s[...], rows).astype(BF16)
            part = dot(rows, wd_v[:, 896 * half : 896 * half + 896])
            e1_s[i, half] = part.astype(BF16).reshape(4, 16, 896)
            for k in range(1, 4):
                out.append(
                    send(
                        e1_s.at[i, half, turn(spots[half], k)], e1_rx.at[i, half, k - 1], rings[half][k],
                        e1_rx.at[i, half, k - 1],
                    )
                )
        return out

    def collect(i, copies):
        arrive(copies)
        for half in range(2):
            total = e1_s[i, half, spots[half]].astype(F32)
            for k in range(3):
                total += e1_rx[i, half, k].astype(F32)
            sum_s[half, 16 * i : 16 * i + 16] = total.astype(BF16)

    wide = [gate_up(0), gate_up(1)]
    thin = [activate(0, wide[0])]
    wide.append(gate_up(2))
    thin.append(activate(1, wide[1]))
    ends = [down(0, thin[0])]
    thin.append(activate(2, wide[2]))
    for i in range(3):
        for j in range(16):
            hid_s[16 * i : 16 * i + 16, 128 * j : 128 * j + 128] = cbuf[i, j % 2, x, j // 4, (j // 2) % 2]
    state = dot(t_s[...], hid_s[...])
    for j in range(16):
        hid_out[:, 112 * j : 112 * j + 112] = state[:, 128 * j : 128 * j + 112]
    ends.append(down(1, thin[1]))
    collect(0, ends[0])
    ends.append(down(2, thin[2]))
    collect(1, ends[1])
    collect(2, ends[2])
    step = []
    for half in range(2):
        e2_s[half] = dot(pad_s[...], sum_s[half]).astype(BF16).reshape(4, 16, 896)
        for k in range(1, 4):
            step.append(
                send(
                    e2_s.at[half, turn(spots[1 - half], k)], e2_rx.at[half, k - 1], rings[1 - half][k],
                    e2_rx.at[half, k - 1],
                )
            )
    arrive(step)
    for half in range(2):
        total = e2_s[half, spots[1 - half]].astype(F32)
        for k in range(3):
            total += e2_rx[half, k].astype(F32)
        u_s[half] = total.reshape(2, 8, 896)
    e3_s[...] = jnp.concatenate([u_s[0, other], u_s[1, other]], axis=0).astype(BF16)
    send(e3_s, e3_rx, zh_dev, e3_rx).wait_recv()
    last = e3_rx[...].astype(F32)
    for half in range(2):
        at = 896 * half
        total = u_s[half, zh] + last[8 * half : 8 * half + 8] + hid_out[:, at : at + 896]
        out_ref[:, at : at + 896] = total[0:6].astype(BF16)
    finish()


def on_device(
    queries, latent_cache, lengths, slot_row, w_uv, w_o, resid, norm_gain, w_gate, w_up, w_down
):
    hbm = pl.BlockSpec(memory_space=pl.ANY)
    vmem = pl.BlockSpec(memory_space=pltpu.VMEM)
    scratch = [
        ((384,), jnp.int32),
        ((7168,), BF16),
        ((64, 128), F32),
        ((6, 32, 576), BF16),
        ((6, 320, 576), BF16),
        ((32, 512, 128), BF16),
        ((2, 112, 384), BF16),
        ((2, 288, 1792), BF16),
        ((2, 288, 1792), BF16),
        ((640, 1792), BF16),
        ((4, 256, 128), F32),
        ((2, 56, 256), F32),
        ((2, 4, 4, 2, 48, 256), BF16),
        ((384, 384), BF16),
        ((192, 4096), BF16),
        ((256, 4096), BF16),
        ((2, 192, 256), BF16),
        ((192, 384), BF16),
        ((192, 256), F32),
        ((3, 4, 16, 256), BF16),
        ((3, 2, 4, 16, 256), BF16),
        ((3, 2, 4, 4, 2, 16, 128), BF16),
        ((48, 2048), BF16),
        ((3, 64, 2048), BF16),
        ((1152, 2048), BF16),
        ((64, 128), F32),
        ((3, 8, 64), F32),
        ((3, 3, 8, 64), F32),
        ((3, 4, 16, 1152), BF16),
        ((3, 3, 16, 1152), BF16),
        ((3, 4, 16, 640), BF16),
        ((64, 64), BF16),
        ((64, 48), BF16),
        ((8, 48), BF16),
        ((8, 1792), F32),
        ((3, 2, 4, 16, 896), BF16),
        ((3, 2, 3, 16, 896), BF16),
        ((2, 48, 896), BF16),
        ((2, 4, 16, 896), BF16),
        ((2, 3, 16, 896), BF16),
        ((2, 2, 8, 896), F32),
        ((16, 896), BF16),
        ((16, 896), BF16),
    ]
    return pl.pallas_call(
        kernel,
        out_shape=jax.ShapeDtypeStruct((6, 1792), BF16),
        in_specs=[hbm] * 11,
        out_specs=vmem,
        scratch_shapes=[pltpu.SMEM((6,), jnp.int32)]
        + [pltpu.VMEM(s, d) for s, d in scratch]
        + [pltpu.SemaphoreType.DMA((SEMS,))],
        compiler_params=pltpu.CompilerParams(
            collective_id=0, has_side_effects=True, vmem_limit_bytes=58 * 1024 * 1024
        ),
        name="layer",
    )(
        queries, latent_cache, lengths, slot_row, w_uv, w_o.T, resid.T, norm_gain, w_gate.T, w_up.T, w_down
    )


def solution(mesh):
    placed = (
        P("dp", "tp", None),
        P("dp", None, None),
        P("dp"),
        P(),
        P("tp", None, None),
        P("tp", "dp"),
        P(None, "dp"),
        P(),
        P("tp", "dp"),
        P("tp", "dp"),
        P("dp", "tp"),
    )
    return jax.shard_map(
        on_device, mesh=mesh, in_specs=placed, out_specs=P("dp", "tp"), check_vma=False
    )
```

```python
import jax
import jax.numpy as jnp
from jax import lax
from jax.experimental import pallas as pl
from jax.experimental.pallas import tpu as pltpu
from jax.sharding import PartitionSpec as P

MESH = pl.DeviceIdType.MESH
F32 = jnp.float32
BF16 = jnp.bfloat16
SCALE = 192.0 ** (-0.5)
SEMS = 88


def iota(shape, axis):
    return lax.broadcasted_iota(jnp.int32, shape, axis)


def by(value, n):
    return ((value.astype(F32) + 0.5) * (1.0 / n)).astype(jnp.int32)


def dot(a, b):
    return jnp.dot(a, b, preferred_element_type=F32)


def dot_t(a, b):
    return lax.dot_general(a, b, (((1,), (1,)), ((), ())), preferred_element_type=F32)


def one_hot(hit):
    return jnp.where(hit, 1.0, 0.0).astype(BF16)


def kernel(
    q_hbm, cache_hbm, len_hbm, slot_hbm, wuv_hbm, wo_hbm, resid_hbm, gain_hbm, wg_hbm, wu_hbm, wd_hbm,
    out_ref,
    len_ref, slot_ref, gain_ref, gain_s,
    q_v, cache_v, wuv_v, resid_v, w_raw, wd_v,
    lat_s, msg_s, abuf, perm_s, z_s, wo_s, slot_s, pt_s, r_s, p_s, b_rx,
    cbuf, hid_s, x_s, w_s, sq_s, ss_s, ss_rx, gu_s, d_rx, act_s,
    turn_s, pad_s, t_s, hid_out,
    e1_s, e1_rx, sum_s, e2_s, e2_rx, u_s, e3_s, e3_rx,
    sems,
):
    dp, t = lax.axis_index("dp"), lax.axis_index("tp")
    c = lax.rem(dp, 2)
    zh = lax.rem(dp // 2, 2)
    y = lax.rem(dp // 4, 4)
    x = dp // 16
    place = dp // 2
    sib = 1 - c
    other = 1 - zh

    def dev(x_, y_, zh_, c_, t_):
        return (((x_ * 4 + y_) * 2 + zh_) * 2 + c_, t_)

    def turn(v, k):
        return lax.rem(v + k + 4, 4)

    used = [0]

    def sem():
        used[0] += 1
        return sems.at[used[0] - 1]

    sends, tails = [], []

    def finish():
        for tail in tails:
            tail()
        for cp in sends:
            cp.wait()

    def remote(src, dst, ss, rs, to):
        return pltpu.make_async_remote_copy(
            src_ref=src, dst_ref=dst, send_sem=ss, recv_sem=rs, device_id=to, device_id_type=MESH
        )

    def group(copies, whole):
        ss, rs = sem(), sem()
        for src, dst, to in copies:
            remote(src, dst, ss, rs, to).start()
        sends.append(pltpu.make_async_copy(whole, whole, ss))
        return landing(whole, rs)

    def landing(whole, rs):
        return pltpu.make_async_copy(whole, whole, rs)

    def send(src, dst, to, lands):
        return group([(src, dst, to)], lands)

    def load(src, dst):
        cp = pltpu.make_async_copy(src, dst, sem())
        cp.start()
        return cp

    sib_dev = dev(x, y, zh, sib, t)
    zh_dev = dev(x, y, other, c, t)
    x_dev = [dev(turn(x, k), y, zh, c, t) for k in range(4)]
    y_dev = [dev(x, turn(y, k), zh, c, t) for k in range(4)]
    t_dev = [(dp, turn(t, k)) for k in range(4)]

    len_in = load(len_hbm, len_ref)
    q_in = load(q_hbm, q_v)
    cache_in = load(cache_hbm, cache_v)
    wuv_in = [load(wuv_hbm.at[pl.ds(16 * i, 16)], wuv_v.at[pl.ds(16 * i, 16)]) for i in range(2)]
    later = [
        load(slot_hbm, slot_ref),
        load(gain_hbm, gain_ref),
        load(resid_hbm, resid_v.at[c]),
        load(wo_hbm, wo_s.at[pl.ds(pl.multiple_of(128 * c, 128), 112)]),
        load(wg_hbm, w_raw.at[0, c]),
        load(wu_hbm, w_raw.at[1, c]),
        load(wd_hbm.at[pl.ds(0, 256)], wd_v.at[pl.ds(pl.multiple_of(256 * c, 256), 256)]),
        load(wd_hbm.at[pl.ds(256, 32)], wd_v.at[pl.ds(pl.multiple_of(512 + 32 * c, 32), 32)]),
    ]
    barrier = pltpu.get_barrier_semaphore()
    for d in [sib_dev, zh_dev] + x_dev[1:] + y_dev[1:] + t_dev[1:]:
        pl.semaphore_signal(barrier, inc=1, device_id=d, device_id_type=MESH)
    for k in range(8):

        @pl.when(jnp.logical_or(x != t, zh * 4 + t != k))
        def _():
            pl.semaphore_signal(
                barrier, inc=1, device_id=dev(t, y, k // 4, c, k % 4), device_id_type=MESH
            )

    for j in range(4):
        lat_s[j, pl.ds(6, 32, 8), :] = jnp.zeros((32, 128), F32)
        lat_s[j, pl.ds(7, 32, 8), :] = jnp.zeros((32, 128), F32)
    len_in.wait()
    q_in.wait()
    cache_in.wait()
    scores = []
    for r in range(6):
        live = iota((32, 320), 1) < len_ref[r]
        scores.append(jnp.where(live, dot_t(q_v[r], cache_v[r]) * SCALE, -1e30))
    scores = jnp.concatenate(scores, axis=0)
    weights = jnp.exp(scores - jnp.max(scores, axis=1, keepdims=True))
    probs = (weights * (1.0 / jnp.sum(weights, axis=1, keepdims=True))).astype(BF16)
    for r in range(6):
        latent = dot(probs[32 * r : 32 * r + 32], cache_v[r, :, :512])
        for j in range(4):
            lat_s[j, pl.ds(r, 32, 8), :] = latent[:, 128 * j : 128 * j + 128]
    for half in range(2):
        wuv_in[half].wait()
        for low in range(8):
            for high in range(2):
                h = half * 16 + low * 2 + high
                latent = [lat_s[j, 8 * h : 8 * h + 8, :].astype(BF16) for j in range(4)]
                value = dot(jnp.concatenate(latent, axis=1), wuv_v[h])
                msg_s[half, 6 * low : 6 * low + 8, 128 * high : 128 * high + 128] = value
        abuf[half, zh, x, y] = msg_s[half, 0:48, :].astype(BF16)

    pl.semaphore_wait(barrier, 19 - jnp.where(x == t, 1, 0))

    every = slice(None)

    def first(block, whole):
        out = []
        for k in range(1, 4):
            out.append((block(0, x, y), block(0, x, y), x_dev[k]))
            out.append((block(1, x, y), block(1, x, y), y_dev[k]))
        return group(out, whole)

    def second(block, whole):
        out = []
        for k in range(1, 4):
            out.append((block(0, every, y), block(0, every, y), y_dev[k]))
            out.append((block(1, x, every), block(1, x, every), x_dev[k]))
        return group(out, whole)

    def near(half, x_, y_):
        return abuf.at[half, zh, x_, y_]

    def far(half, x_, y_):
        return abuf.at[half, other, x_, y_]

    six, twenty_four = abuf.at[0, 0, 0:3, 0:2], abuf.at[0:2, 0, 0:3]
    near_in = first(near, six)
    far_in = send(abuf.at[:, zh, x, y], abuf.at[:, zh, x, y], zh_dev, abuf.at[:, other, x, y])
    for cp in later:
        cp.wait()
    theirs = [
        send(resid_v.at[c], resid_v.at[c], sib_dev, resid_v.at[sib]),
        send(w_raw.at[:, c], w_raw.at[:, c], sib_dev, w_raw.at[:, sib]),
    ]
    for ref, at, step_, n in ((wo_s, 0, 128, 112), (wd_v, 0, 256, 256), (wd_v, 512, 32, 32)):
        ours = ref.at[pl.ds(pl.multiple_of(at + step_ * c, step_), n)]
        other_half = ref.at[pl.ds(pl.multiple_of(at + step_ * sib, step_), n)]
        theirs.append(send(ours, ours, sib_dev, other_half))
    row, col = iota((384, 384), 0), iota((384, 384), 1)
    low = by(row, 48)
    within = row - 48 * low
    source = by(within, 6)
    perm_s[...] = one_hot(col == source * 48 + low * 6 + (within - 6 * source))
    near_in.wait()
    near_in = second(near, twenty_four)

    half_of = jnp.where(col >= 192, 1, 0)
    rho = col - 192 * half_of
    z_of = jnp.where(rho >= 96, 1, 0)
    rho -= 96 * z_of
    chip = by(rho, 6)
    order = one_hot(row == ((chip * 2 + z_of) * 2 + half_of) * 6 + (rho - 6 * chip))
    line = iota((192, 384), 0)
    want = ((line % 64) // 2 * 2 + c) * 6 + line // 64 * 2 + line % 2
    slots = jnp.broadcast_to(slot_ref[...][None, :], (192, 384))
    pt_s[...] = dot(one_hot(slots == want), order).astype(BF16)
    rows_here = one_hot(iota((192, 384), 1) == want)
    far_in.wait()
    far_in = first(far, six)

    for cp in theirs:
        cp.wait()
    r_s[...] = jnp.zeros((192, 256), F32)
    for k in range(2):
        r_s[:, 128 * k : 128 * k + 112] = dot_t(rows_here, resid_v[k])
        wo_s[128 * k + 112 : 128 * k + 128, :] = jnp.zeros((16, 4096), BF16)
    gain_s[...] = jnp.zeros((64, 128), F32)
    gains = gain_ref[...].astype(F32)[None, :]
    for j in range(64):
        gain_s[j : j + 1, 0:112] = gains[:, 112 * j : 112 * j + 112]
    line, row = iota((64, 64), 0), iota((64, 64), 1)
    turn_s[...] = one_hot(row == line // 4 % 4 * 16 + line // 16 * 4 + line % 4)
    line, row = iota((64, 48), 0), iota((64, 48), 1)
    pad_s[...] = one_hot(
        jnp.logical_and(line % 8 < 6, row == line % 8 // 2 * 16 + line // 8 * 2 + line % 2)
    )
    line, row = iota((8, 48), 0), iota((8, 48), 1)
    t_s[...] = one_hot(jnp.logical_and(line < 6, row == line // 2 * 16 + (y * 2 + zh) * 2 + line % 2))
    wd_v[576:640, :] = jnp.zeros((64, 1792), BF16)
    far_in.wait()
    far_in = second(far, twenty_four)

    def spread(block, part, at):
        width = block.shape[1]
        for j in range(8):
            row = 1024 * part + 128 * j
            w_s[row : row + 112, at : at + width] = block[112 * j : 112 * j + 112]

    for j in range(16):
        w_s[128 * j + 112 : 128 * j + 128, :] = jnp.zeros((16, 1152), BF16)
    for part in range(2):
        cols = slice(896 * part, 896 * part + 896)
        for k in range(2):
            for half in range(2):
                spread(w_raw[k, half, 0:256, cols].T, part, 512 * k + 256 * half)
        rest = [w_raw[k, half, 256:288, cols] for k in range(2) for half in range(2)]
        spread(jnp.concatenate(rest, axis=0).T, part, 1024)

    def project(z_):
        for half in range(2):
            for k in range(2):
                packed = abuf[half, z_, 2 * k : 2 * k + 2].reshape(384, 256)
                placed = dot(perm_s[...], packed).astype(BF16)
                for low in range(8):
                    at = half * 2048 + low * 256
                    z_s[48 * k : 48 * k + 48, at : at + 256] = placed[48 * low : 48 * low + 48]
        slot_s[c, z_] = dot_t(z_s[...], wo_s[...]).astype(BF16)
        return send(slot_s.at[c, z_], slot_s.at[c, z_], sib_dev, slot_s.at[sib, z_])

    near_in.wait()
    step = [project(zh)]
    far_in.wait()
    step.append(project(other))
    for cp in step:
        cp.wait()
    partial = dot(pt_s[...], slot_s[...].reshape(384, 256)) + jnp.where(t == 0, r_s[...], 0.0)
    p_s[...] = partial.astype(BF16).reshape(12, 16, 256)

    b_sent, b_in = sem(), [sem() for _ in range(3)]
    for i in range(3):
        for k in range(4):
            for z_ in range(2):
                own = jnp.logical_and(jnp.logical_and(x == t, k == x), zh == z_)
                src, dst = p_s.at[4 * i + k], b_rx.at[8 * i + 4 * zh + t]

                @pl.when(jnp.logical_not(own))
                def _():
                    remote(src, dst, b_sent, b_in[i], dev(k, y, z_, c, x)).start()

                @pl.when(own)
                def _():
                    pltpu.make_async_copy(src, dst, b_in[i]).start()

    def sent():
        for n, when in ((24, x != t), (21, x == t)):

            @pl.when(when)
            def _():
                pltpu.make_async_copy(b_rx.at[0:n], b_rx.at[0:n], b_sent).wait()

    tails.append(sent)

    def blocks(i):
        def block(half, x_, y_):
            return cbuf.at[i, half, x_, y_]

        return block

    step = []
    for i in range(3):
        landing(b_rx.at[8 * i : 8 * i + 8], b_in[i]).wait()
        for z_ in range(2):
            at = 8 * i + 4 * z_
            hidden = jnp.sum(b_rx[at : at + 4].astype(F32), axis=0).astype(BF16)
            for half in range(2):
                cbuf[i, half, x, y, z_] = hidden[:, 128 * half : 128 * half + 128]
        step.append(first(blocks(i), cbuf.at[i, 0, 0:3, 0:2]))
    for i in range(3):
        step[i].wait()
        step[i] = second(blocks(i), cbuf.at[i, 0:2, 0:3])

    gain = gain_s[pl.ds(pl.multiple_of(16 * t, 16), 16), :]

    def silu(v):
        return v * jax.nn.sigmoid(v)

    def gate_up(i):
        step[i].wait()
        for k in range(4):
            squares = jnp.zeros((16, 128), F32)
            for j in range(16):
                block = cbuf[i, j % 2, k, j // 4, (j // 2) % 2].astype(F32)
                squares += block * block
                x_s[i, 16 * k : 16 * k + 16, 128 * j : 128 * j + 128] = (block * gain[j : j + 1]).astype(BF16)
            sq_s[16 * k : 16 * k + 16] = squares
        ss_s[i] = lax.dot_general(
            jnp.ones((8, 128), F32), sq_s[...], (((1,), (1,)), ((), ())),
            precision=lax.Precision.HIGHEST, preferred_element_type=F32,
        )
        out = [group([(ss_s.at[i], ss_rx.at[i, k - 1], t_dev[k]) for k in range(1, 4)], ss_rx.at[i])]
        gu_s[i] = dot(x_s[i], w_s[...]).astype(BF16).reshape(4, 16, 1152)
        parts = [(gu_s.at[i, turn(t, k)], d_rx.at[i, k - 1], t_dev[k]) for k in range(1, 4)]
        out.append(group(parts, d_rx.at[i]))
        return out

    def activate(i, copies):
        for cp in copies:
            cp.wait()
        total = gu_s[i, t].astype(F32)
        squares = ss_s[i]
        for k in range(3):
            total += d_rx[i, k].astype(F32)
            squares += ss_rx[i, k]
        here = iota((16, 64), 1) == 16 * t + iota((16, 64), 0)
        squares = jnp.sum(jnp.where(here, squares[0:1], 0.0), axis=1, keepdims=True)
        total *= lax.rsqrt(squares * (1.0 / 7168) + 1e-06)
        rest = total[:, 1024:1152]
        tail = silu(rest) * pltpu.roll(rest, 64, 1)
        act_s[i, t, :, 0:512] = (silu(total[:, 0:512]) * total[:, 512:1024]).astype(BF16)
        act_s[i, t, :, 512:640] = jnp.where(iota((16, 128), 1) < 64, tail, 0.0).astype(BF16)
        mine = act_s.at[i, t]
        return group([(mine, mine, t_dev[k]) for k in range(1, 4)], act_s.at[i, 0:3])

    spots = (x, y)
    rings = (x_dev, y_dev)

    def down(i, copies):
        copies.wait()
        rows = act_s[i].reshape(64, 640)
        out = []
        for half in range(2):
            if half == 1:
                rows = dot(turn_s[...], rows).astype(BF16)
            part = dot(rows, wd_v[:, 896 * half : 896 * half + 896])
            e1_s[i, half] = part.astype(BF16).reshape(4, 16, 896)
            for k in range(1, 4):
                out.append((e1_s.at[i, half, turn(spots[half], k)], e1_rx.at[i, half, k - 1], rings[half][k]))
        return group(out, e1_rx.at[i])

    def collect(i, copies):
        copies.wait()
        for half in range(2):
            total = e1_s[i, half, spots[half]].astype(F32)
            for k in range(3):
                total += e1_rx[i, half, k].astype(F32)
            sum_s[half, 16 * i : 16 * i + 16] = total.astype(BF16)

    wide = [gate_up(i) for i in range(3)]
    for i in range(3):
        for j in range(16):
            hid_s[16 * i : 16 * i + 16, 128 * j : 128 * j + 128] = cbuf[i, j % 2, x, j // 4, (j // 2) % 2]
    state = dot(t_s[...], hid_s[...])
    for j in range(16):
        hid_out[:, 112 * j : 112 * j + 112] = state[:, 128 * j : 128 * j + 112]
    thin = [activate(i, wide[i]) for i in range(3)]
    ends = [down(0, thin[0]), down(1, thin[1])]
    collect(0, ends[0])
    ends.append(down(2, thin[2]))
    collect(1, ends[1])
    collect(2, ends[2])
    step = []
    for half in range(2):
        e2_s[half] = dot(pad_s[...], sum_s[half]).astype(BF16).reshape(4, 16, 896)
        for k in range(1, 4):
            to = rings[1 - half][k]
            step.append((e2_s.at[half, turn(spots[1 - half], k)], e2_rx.at[half, k - 1], to))
    group(step, e2_rx).wait()
    for half in range(2):
        total = e2_s[half, spots[1 - half]].astype(F32)
        for k in range(3):
            total += e2_rx[half, k].astype(F32)
        u_s[half] = total.reshape(2, 8, 896)
    e3_s[...] = jnp.concatenate([u_s[0, other], u_s[1, other]], axis=0).astype(BF16)
    send(e3_s, e3_rx, zh_dev, e3_rx).wait()
    last = e3_rx[...].astype(F32)
    for half in range(2):
        at = 896 * half
        total = u_s[half, zh] + last[8 * half : 8 * half + 8] + hid_out[:, at : at + 896]
        out_ref[:, at : at + 896] = total[0:6].astype(BF16)
    finish()


def on_device(
    queries, latent_cache, lengths, slot_row, w_uv, w_o, resid, norm_gain, w_gate, w_up, w_down
):
    hbm = pl.BlockSpec(memory_space=pl.ANY)
    vmem = pl.BlockSpec(memory_space=pltpu.VMEM)
    scratch = [
        ((384,), jnp.int32),
        ((7168,), BF16),
        ((64, 128), F32),
        ((6, 32, 576), BF16),
        ((6, 320, 576), BF16),
        ((32, 512, 128), BF16),
        ((2, 112, 384), BF16),
        ((2, 2, 288, 1792), BF16),
        ((640, 1792), BF16),
        ((4, 256, 128), F32),
        ((2, 56, 256), F32),
        ((2, 2, 4, 4, 48, 256), BF16),
        ((384, 384), BF16),
        ((96, 4096), BF16),
        ((256, 4096), BF16),
        ((2, 2, 96, 256), BF16),
        ((192, 384), BF16),
        ((192, 256), F32),
        ((12, 16, 256), BF16),
        ((24, 16, 256), BF16),
        ((3, 2, 4, 4, 2, 16, 128), BF16),
        ((48, 2048), BF16),
        ((3, 64, 2048), BF16),
        ((2048, 1152), BF16),
        ((64, 128), F32),
        ((3, 8, 64), F32),
        ((3, 3, 8, 64), F32),
        ((3, 4, 16, 1152), BF16),
        ((3, 3, 16, 1152), BF16),
        ((3, 4, 16, 640), BF16),
        ((64, 64), BF16),
        ((64, 48), BF16),
        ((8, 48), BF16),
        ((8, 1792), F32),
        ((3, 2, 4, 16, 896), BF16),
        ((3, 2, 3, 16, 896), BF16),
        ((2, 48, 896), BF16),
        ((2, 4, 16, 896), BF16),
        ((2, 3, 16, 896), BF16),
        ((2, 2, 8, 896), F32),
        ((16, 896), BF16),
        ((16, 896), BF16),
    ]
    return pl.pallas_call(
        kernel,
        out_shape=jax.ShapeDtypeStruct((6, 1792), BF16),
        in_specs=[hbm] * 11,
        out_specs=vmem,
        scratch_shapes=[pltpu.SMEM((6,), jnp.int32)]
        + [pltpu.VMEM(s, d) for s, d in scratch]
        + [pltpu.SemaphoreType.DMA((SEMS,))],
        compiler_params=pltpu.CompilerParams(
            collective_id=0, has_side_effects=True, vmem_limit_bytes=58 * 1024 * 1024
        ),
        name="layer",
    )(
        queries, latent_cache, lengths, slot_row, w_uv, w_o.T, resid.T, norm_gain, w_gate.T, w_up.T, w_down
    )


def solution(mesh):
    placed = (
        P("dp", "tp", None),
        P("dp", None, None),
        P("dp"),
        P(),
        P("tp", None, None),
        P("tp", "dp"),
        P(None, "dp"),
        P(),
        P("tp", "dp"),
        P("tp", "dp"),
        P("dp", "tp"),
    )
    return jax.shard_map(
        on_device, mesh=mesh, in_specs=placed, out_specs=P("dp", "tp"), check_vma=False
    )
```

```python
import jax
import jax.numpy as jnp
from jax import lax
from jax.experimental import pallas as pl
from jax.experimental.pallas import tpu as pltpu
from jax.sharding import PartitionSpec as P

MESH = pl.DeviceIdType.MESH
F32 = jnp.float32
BF16 = jnp.bfloat16
SCALE = 192.0 ** (-0.5)
SEMS = 108


def iota(shape, axis):
    return lax.broadcasted_iota(jnp.int32, shape, axis)


def by(value, n):
    return ((value.astype(F32) + 0.5) * (1.0 / n)).astype(jnp.int32)


def dot(a, b):
    return jnp.dot(a, b, preferred_element_type=F32)


def dot_t(a, b):
    return lax.dot_general(a, b, (((1,), (1,)), ((), ())), preferred_element_type=F32)


def one_hot(hit):
    return jnp.where(hit, 1.0, 0.0).astype(BF16)


def kernel(
    q_hbm, cache_hbm, len_hbm, slot_hbm, wuv_hbm, wo_hbm, resid_hbm, gain_hbm, wg_hbm, wu_hbm, wd_hbm,
    out_ref,
    len_ref, slot_ref, gain_ref, gain_s,
    q_v, cache_v, wuv_v, resid_v, w_raw, wd_v,
    lat_s, msg_s, abuf, perm_s, z_s, wo_s, r_s, p_s, b_rx,
    cbuf, hid_s, x_s, w_s, sq_s, ss_s, ss_rx, gu_s, d_rx, act_s,
    pt_s, pad_s, t_s, hm_s, hm_rx, hid_out,
    e1_s, e1_rx, sum_s, e2_s, e2_rx, u_s, e3_s, e3_rx,
    sems,
):
    dp, t = lax.axis_index("dp"), lax.axis_index("tp")
    c = lax.rem(dp, 2)
    zh = lax.rem(dp // 2, 2)
    y = lax.rem(dp // 4, 4)
    x = dp // 16
    place = dp // 2
    sib = 1 - c
    other = 1 - zh

    def dev(x_, y_, zh_, c_, t_):
        return (((x_ * 4 + y_) * 2 + zh_) * 2 + c_, t_)

    def turn(v, k):
        return lax.rem(v + k + 4, 4)

    used = [0]

    def sem():
        used[0] += 1
        return sems.at[used[0] - 1]

    sends, tails = [], []

    def finish():
        for tail in tails:
            tail()
        for cp in sends:
            cp.wait()

    def remote(src, dst, ss, rs, to):
        return pltpu.make_async_remote_copy(
            src_ref=src, dst_ref=dst, send_sem=ss, recv_sem=rs, device_id=to, device_id_type=MESH
        )

    def group(copies, whole):
        ss, rs = sem(), sem()
        for src, dst, to in copies:
            remote(src, dst, ss, rs, to).start()
        sends.append(pltpu.make_async_copy(whole, whole, ss))
        return landing(whole, rs)

    def landing(whole, rs):
        return pltpu.make_async_copy(whole, whole, rs)

    def send(src, dst, to, lands):
        return group([(src, dst, to)], lands)

    def load(src, dst):
        cp = pltpu.make_async_copy(src, dst, sem())
        cp.start()
        return cp

    sib_dev = dev(x, y, zh, sib, t)
    zh_dev = dev(x, y, other, c, t)
    x_dev = [dev(turn(x, k), y, zh, c, t) for k in range(4)]
    y_dev = [dev(x, turn(y, k), zh, c, t) for k in range(4)]
    t_dev = [(dp, turn(t, k)) for k in range(4)]

    len_in = load(len_hbm, len_ref)
    q_in = load(q_hbm, q_v)
    cache_in = load(cache_hbm, cache_v)
    wuv_in = [load(wuv_hbm.at[pl.ds(16 * i, 16)], wuv_v.at[pl.ds(16 * i, 16)]) for i in range(2)]
    later = [
        load(slot_hbm, slot_ref),
        load(gain_hbm, gain_ref),
        load(resid_hbm, resid_v.at[c]),
        load(wo_hbm, wo_s.at[pl.ds(pl.multiple_of(128 * c, 128), 112)]),
        load(wg_hbm, w_raw.at[0, c]),
        load(wu_hbm, w_raw.at[1, c]),
        load(wd_hbm.at[pl.ds(0, 256)], wd_v.at[pl.ds(pl.multiple_of(256 * c, 256), 256)]),
        load(wd_hbm.at[pl.ds(256, 32)], wd_v.at[pl.ds(pl.multiple_of(512 + 32 * c, 32), 32)]),
    ]
    barrier = pltpu.get_barrier_semaphore()
    for d in [sib_dev, zh_dev] + x_dev[1:] + y_dev[1:] + t_dev[1:]:
        pl.semaphore_signal(barrier, inc=1, device_id=d, device_id_type=MESH)
    for k in range(8):

        @pl.when(jnp.logical_or(x != t, zh * 4 + t != k))
        def _():
            pl.semaphore_signal(
                barrier, inc=1, device_id=dev(t, y, k // 4, c, k % 4), device_id_type=MESH
            )

    for j in range(4):
        lat_s[j, pl.ds(6, 32, 8), :] = jnp.zeros((32, 128), F32)
        lat_s[j, pl.ds(7, 32, 8), :] = jnp.zeros((32, 128), F32)
    len_in.wait()
    q_in.wait()
    cache_in.wait()
    scores = []
    for r in range(6):
        live = iota((32, 320), 1) < len_ref[r]
        scores.append(jnp.where(live, dot_t(q_v[r], cache_v[r]) * SCALE, -1e30))
    scores = jnp.concatenate(scores, axis=0)
    weights = jnp.exp(scores - jnp.max(scores, axis=1, keepdims=True))
    probs = (weights * (1.0 / jnp.sum(weights, axis=1, keepdims=True))).astype(BF16)
    for r in range(6):
        latent = dot(probs[32 * r : 32 * r + 32], cache_v[r, :, :512])
        for j in range(4):
            lat_s[j, pl.ds(r, 32, 8), :] = latent[:, 128 * j : 128 * j + 128]
    for half in range(2):
        wuv_in[half].wait()
        for low in range(8):
            for high in range(2):
                h = half * 16 + low * 2 + high
                latent = [lat_s[j, 8 * h : 8 * h + 8, :].astype(BF16) for j in range(4)]
                value = dot(jnp.concatenate(latent, axis=1), wuv_v[h])
                for i in range(3):
                    msg_s[i, half, 2 * low : 2 * low + 2, 128 * high : 128 * high + 128] = value[2 * i : 2 * i + 2]
    for i in range(3):
        for half in range(2):
            abuf[i, half, zh, x, y] = msg_s[i, half].astype(BF16)

    pl.semaphore_wait(barrier, 19 - jnp.where(x == t, 1, 0))

    every = slice(None)

    def first(block, whole):
        out = []
        for k in range(1, 4):
            out.append((block(0, x, y), block(0, x, y), x_dev[k]))
            out.append((block(1, x, y), block(1, x, y), y_dev[k]))
        return group(out, whole)

    def second(block, whole):
        out = []
        for k in range(1, 4):
            out.append((block(0, every, y), block(0, every, y), y_dev[k]))
            out.append((block(1, x, every), block(1, x, every), x_dev[k]))
        return group(out, whole)

    def values_at(i, z_):
        def block(half, x_, y_):
            return abuf.at[i, half, z_, x_, y_]

        return block

    def near_second(i):
        near_in[i].wait()
        near_in[i] = second(values_at(i, zh), abuf.at[i, 0:2, 0, 0:3])

    def far_first(i):
        far_in[i].wait()
        far_in[i] = first(values_at(i, other), abuf.at[i, 0, 0, 0:3, 0:2])

    def far_second(i):
        far_in[i].wait()
        far_in[i] = second(values_at(i, other), abuf.at[i, 0:2, 0, 0:3])

    near_in, far_in = [], []
    for i in range(3):
        mine = abuf.at[i, :, zh, x, y]
        far_in.append(send(mine, mine, zh_dev, abuf.at[i, :, other, x, y]))
        near_in.append(first(values_at(i, zh), abuf.at[i, 0, 0, 0:3, 0:2]))
    for cp in later:
        cp.wait()
    theirs = [
        send(resid_v.at[c], resid_v.at[c], sib_dev, resid_v.at[sib]),
        send(w_raw.at[:, c], w_raw.at[:, c], sib_dev, w_raw.at[:, sib]),
    ]
    for ref, at, step_, n in ((wo_s, 0, 128, 112), (wd_v, 0, 256, 256), (wd_v, 512, 32, 32)):
        ours = ref.at[pl.ds(pl.multiple_of(at + step_ * c, step_), n)]
        other_half = ref.at[pl.ds(pl.multiple_of(at + step_ * sib, step_), n)]
        theirs.append(send(ours, ours, sib_dev, other_half))
    row, col = iota((256, 256), 0), iota((256, 256), 1)
    perm_s[...] = one_hot(col == row % 32 // 2 * 16 + row // 32 * 2 + row % 2)
    near_second(0)
    near_second(1)
    far_first(0)
    far_first(1)
    far_first(2)
    near_second(2)

    def slot_at(core, line):
        chip = line % 32 // 2 * 2 + line % 64 // 32
        return (chip * 2 + core) * 6 + line // 64 * 2 + line % 2

    order_c = one_hot(iota((192, 384), 1) == slot_at(c, iota((192, 384), 0)))
    slots = jnp.broadcast_to(slot_ref[...][None, :], (384, 384))
    moved = dot_t(order_c, one_hot(slots == iota((384, 384), 0))).astype(BF16)
    for cp in theirs:
        cp.wait()
    r_s[...] = jnp.zeros((192, 256), F32)
    for k in range(2):
        r_s[:, 128 * k : 128 * k + 112] = dot_t(moved, resid_v[k])
        wo_s[128 * k + 112 : 128 * k + 128, :] = jnp.zeros((16, 4096), BF16)
    far_second(0)
    far_second(1)
    far_second(2)

    def project(i):
        near_in[i].wait()
        far_in[i].wait()
        for z_ in range(2):
            for half in range(2):
                placed = dot(perm_s[...], abuf[i, half, z_].reshape(256, 256)).astype(BF16)
                for low in range(8):
                    at = half * 2048 + low * 256
                    z_s[32 * z_ : 32 * z_ + 32, at : at + 256] = placed[32 * low : 32 * low + 32]
        partial = dot_t(z_s[...], wo_s[...]) + jnp.where(t == 0, r_s[64 * i : 64 * i + 64], 0.0)
        p_s[4 * i : 4 * i + 4] = partial.astype(BF16).reshape(4, 16, 256)

    b_sent, b_in = sem(), [sem() for _ in range(3)]
    own = x == t

    def deal(i):
        for k in range(4):
            for z_ in range(2):
                src, dst = p_s.at[4 * i + turn(x, k)], b_rx.at[8 * i + 4 * zh + t]
                to = dev(turn(x, k), y, lax.rem(zh + z_, 2), c, x)
                if k + z_ > 0:
                    remote(src, dst, b_sent, b_in[i], to).start()
                else:

                    @pl.when(jnp.logical_not(own))
                    def _():
                        remote(src, dst, b_sent, b_in[i], to).start()

                    @pl.when(own)
                    def _():
                        pltpu.make_async_copy(src, dst, b_in[i]).start()

    def sent():
        for n, when in ((24, jnp.logical_not(own)), (21, own)):

            @pl.when(when)
            def _():
                pltpu.make_async_copy(b_rx.at[0:n], b_rx.at[0:n], b_sent).wait()

    tails.append(sent)
    for i in range(3):
        project(i)
        deal(i)

    def spread(block, part, at):
        width = block.shape[1]
        for j in range(8):
            row = 1024 * part + 128 * j
            w_s[row : row + 112, at : at + width] = block[112 * j : 112 * j + 112]

    for j in range(16):
        w_s[128 * j + 112 : 128 * j + 128, :] = jnp.zeros((16, 1152), BF16)
    for part in range(2):
        cols = slice(896 * part, 896 * part + 896)
        for k in range(2):
            for half in range(2):
                spread(w_raw[k, half, 0:256, cols].T, part, 512 * k + 256 * half)
        rest = [w_raw[k, half, 256:288, cols] for k in range(2) for half in range(2)]
        spread(jnp.concatenate(rest, axis=0).T, part, 1024)
    gain_s[...] = jnp.zeros((64, 128), F32)
    gains = gain_ref[...].astype(F32)[None, :]
    for j in range(64):
        gain_s[j : j + 1, 0:112] = gains[:, 112 * j : 112 * j + 112]

    def blocks(i):
        def block(half, x_, y_):
            return cbuf.at[i, half, x_, y_]

        return block

    def hidden_first(i):
        landing(b_rx.at[8 * i : 8 * i + 8], b_in[i]).wait()
        for z_ in range(2):
            at = 8 * i + 4 * z_
            hidden = jnp.sum(b_rx[at : at + 4].astype(F32), axis=0).astype(BF16)
            for half in range(2):
                cbuf[i, half, x, y, z_] = hidden[:, 128 * half : 128 * half + 128]
        step.append(first(blocks(i), cbuf.at[i, 0, 0:3, 0:2]))

    def hidden_second(i):
        step[i].wait()
        step[i] = second(blocks(i), cbuf.at[i, 0:2, 0:3])

    step = []
    hidden_first(0)
    hidden_first(1)
    hidden_second(0)
    hidden_first(2)
    hidden_second(1)
    hidden_second(2)

    gain = gain_s[pl.ds(pl.multiple_of(16 * t, 16), 16), :]

    def silu(v):
        return v * jax.nn.sigmoid(v)

    def gate_up(i):
        step[i].wait()
        for k in range(4):
            squares = jnp.zeros((16, 128), F32)
            for j in range(16):
                block = cbuf[i, j % 2, k, j // 4, (j // 2) % 2]
                hid_s[64 * i + 16 * k : 64 * i + 16 * k + 16, 128 * j : 128 * j + 128] = block
                block = block.astype(F32)
                squares += block * block
                x_s[i, 16 * k : 16 * k + 16, 128 * j : 128 * j + 128] = (block * gain[j : j + 1]).astype(BF16)
            sq_s[16 * k : 16 * k + 16] = squares
        ss_s[i] = lax.dot_general(
            jnp.ones((8, 128), F32), sq_s[...], (((1,), (1,)), ((), ())),
            precision=lax.Precision.HIGHEST, preferred_element_type=F32,
        )
        out = [group([(ss_s.at[i], ss_rx.at[i, k - 1], t_dev[k]) for k in range(1, 4)], ss_rx.at[i])]
        gu_s[i] = dot(x_s[i], w_s[...]).astype(BF16).reshape(4, 16, 1152)
        parts = [(gu_s.at[i, turn(t, k)], d_rx.at[i, k - 1], t_dev[k]) for k in range(1, 4)]
        out.append(group(parts, d_rx.at[i]))
        return out

    def activate(i, copies):
        for cp in copies:
            cp.wait()
        total = gu_s[i, t].astype(F32)
        squares = ss_s[i]
        for k in range(3):
            total += d_rx[i, k].astype(F32)
            squares += ss_rx[i, k]
        here = iota((16, 64), 1) == 16 * t + iota((16, 64), 0)
        squares = jnp.sum(jnp.where(here, squares[0:1], 0.0), axis=1, keepdims=True)
        total *= lax.rsqrt(squares * (1.0 / 7168) + 1e-06)
        rest = total[:, 1024:1152]
        tail = silu(rest) * pltpu.roll(rest, 64, 1)
        act_s[c, i, t, :, 0:512] = (silu(total[:, 0:512]) * total[:, 512:1024]).astype(BF16)
        act_s[c, i, t, :, 512:640] = jnp.where(iota((16, 128), 1) < 64, tail, 0.0).astype(BF16)
        mine = act_s.at[c, i, t]
        return group([(mine, mine, t_dev[k]) for k in range(1, 4)], act_s.at[0, i, 0:3])

    def share(i, copies):
        copies.wait()
        return send(act_s.at[c, i], act_s.at[c, i], sib_dev, act_s.at[sib, i])

    spots = (x, y)
    rings = (x_dev, y_dev)

    wide = [gate_up(i) for i in range(3)]
    line = iota((16, 384), 0)
    want = jnp.where(line % 8 < 6, (place * 2 + line // 8) * 6 + line % 8, -1)
    t_s[...] = dot_t(one_hot(slots[:16] == want), order_c).astype(BF16)
    hm_s[...] = dot(t_s[...], hid_s[...]).reshape(2, 8, 2048)
    hm_in = send(hm_s.at[sib], hm_rx, sib_dev, hm_rx)
    col = iota((384, 384), 1)
    core = jnp.where(col >= 192, 1, 0)
    order = one_hot(iota((384, 384), 0) == slot_at(core, col - 192 * core))
    line = iota((192, 384), 0)
    chip = by(line, 6)
    line -= 6 * chip
    pt_s[0] = dot(one_hot(slots[:192] == 12 * chip + 6 * c + line), order).astype(BF16)
    chip = (chip // 2 % 4 * 4 + chip // 8) * 2 + chip % 2
    pt_s[1] = dot(one_hot(slots[:192] == 12 * chip + 6 * c + line), order).astype(BF16)
    line, row = iota((64, 48), 0), iota((64, 48), 1)
    pad_s[...] = one_hot(jnp.logical_and(line % 8 < 6, row == line // 8 * 6 + line % 8))
    wd_v[576:640, :] = jnp.zeros((64, 1792), BF16)
    hm_in.wait()
    state = hm_s[c] + hm_rx[...]
    for j in range(16):
        hid_out[:, 112 * j : 112 * j + 112] = state[:, 128 * j : 128 * j + 112]
    thin = [activate(i, wide[i]) for i in range(3)]
    ends = [share(i, thin[i]) for i in range(3)]
    for cp in ends:
        cp.wait()

    everyone = act_s[...].reshape(384, 640)
    step = []
    for half in range(2):
        rows = dot(pt_s[half], everyone).astype(BF16)
        part = dot(rows, wd_v[:, 896 * half : 896 * half + 896])
        e1_s[half] = part.astype(BF16).reshape(4, 48, 896)
        parts = [
            (e1_s.at[half, turn(spots[half], k)], e1_rx.at[half, k - 1], rings[half][k]) for k in range(1, 4)
        ]
        step.append(group(parts, e1_rx.at[half]))
    for half in range(2):
        step[half].wait()
        total = e1_s[half, spots[half]].astype(F32)
        for k in range(3):
            total += e1_rx[half, k].astype(F32)
        sum_s[half] = total.astype(BF16)
    step = []
    for half in range(2):
        e2_s[half] = dot(pad_s[...], sum_s[half]).astype(BF16).reshape(4, 16, 896)
        for k in range(1, 4):
            to = rings[1 - half][k]
            step.append((e2_s.at[half, turn(spots[1 - half], k)], e2_rx.at[half, k - 1], to))
    group(step, e2_rx).wait()
    for half in range(2):
        total = e2_s[half, spots[1 - half]].astype(F32)
        for k in range(3):
            total += e2_rx[half, k].astype(F32)
        u_s[half] = total.reshape(2, 8, 896)
    e3_s[...] = jnp.concatenate([u_s[0, other], u_s[1, other]], axis=0).astype(BF16)
    send(e3_s, e3_rx, zh_dev, e3_rx).wait()
    last = e3_rx[...].astype(F32)
    for half in range(2):
        at = 896 * half
        total = u_s[half, zh] + last[8 * half : 8 * half + 8] + hid_out[:, at : at + 896]
        out_ref[:, at : at + 896] = total[0:6].astype(BF16)
    finish()


def on_device(
    queries, latent_cache, lengths, slot_row, w_uv, w_o, resid, norm_gain, w_gate, w_up, w_down
):
    hbm = pl.BlockSpec(memory_space=pl.ANY)
    vmem = pl.BlockSpec(memory_space=pltpu.VMEM)
    scratch = [
        ((384,), jnp.int32),
        ((7168,), BF16),
        ((64, 128), F32),
        ((6, 32, 576), BF16),
        ((6, 320, 576), BF16),
        ((32, 512, 128), BF16),
        ((2, 112, 384), BF16),
        ((2, 2, 288, 1792), BF16),
        ((640, 1792), BF16),
        ((4, 256, 128), F32),
        ((3, 2, 16, 256), F32),
        ((3, 2, 2, 4, 4, 16, 256), BF16),
        ((256, 256), BF16),
        ((64, 4096), BF16),
        ((256, 4096), BF16),
        ((192, 256), F32),
        ((12, 16, 256), BF16),
        ((24, 16, 256), BF16),
        ((3, 2, 4, 4, 2, 16, 128), BF16),
        ((192, 2048), BF16),
        ((3, 64, 2048), BF16),
        ((2048, 1152), BF16),
        ((64, 128), F32),
        ((3, 8, 64), F32),
        ((3, 3, 8, 64), F32),
        ((3, 4, 16, 1152), BF16),
        ((3, 3, 16, 1152), BF16),
        ((2, 3, 4, 16, 640), BF16),
        ((2, 192, 384), BF16),
        ((64, 48), BF16),
        ((16, 192), BF16),
        ((2, 8, 2048), F32),
        ((8, 2048), F32),
        ((8, 1792), F32),
        ((2, 4, 48, 896), BF16),
        ((2, 3, 48, 896), BF16),
        ((2, 48, 896), BF16),
        ((2, 4, 16, 896), BF16),
        ((2, 3, 16, 896), BF16),
        ((2, 2, 8, 896), F32),
        ((16, 896), BF16),
        ((16, 896), BF16),
    ]
    return pl.pallas_call(
        kernel,
        out_shape=jax.ShapeDtypeStruct((6, 1792), BF16),
        in_specs=[hbm] * 11,
        out_specs=vmem,
        scratch_shapes=[pltpu.SMEM((6,), jnp.int32)]
        + [pltpu.VMEM(s, d) for s, d in scratch]
        + [pltpu.SemaphoreType.DMA((SEMS,))],
        compiler_params=pltpu.CompilerParams(
            collective_id=0, has_side_effects=True, vmem_limit_bytes=58 * 1024 * 1024
        ),
        name="layer",
    )(
        queries, latent_cache, lengths, slot_row, w_uv, w_o.T, resid.T, norm_gain, w_gate.T, w_up.T, w_down
    )


def solution(mesh):
    placed = (
        P("dp", "tp", None),
        P("dp", None, None),
        P("dp"),
        P(),
        P("tp", None, None),
        P("tp", "dp"),
        P(None, "dp"),
        P(),
        P("tp", "dp"),
        P("tp", "dp"),
        P("dp", "tp"),
    )
    return jax.shard_map(
        on_device, mesh=mesh, in_specs=placed, out_specs=P("dp", "tp"), check_vma=False
    )
```

```python
import jax
import jax.numpy as jnp
from jax import lax
from jax.experimental import pallas as pl
from jax.experimental.pallas import tpu as pltpu
from jax.sharding import PartitionSpec as P

MESH = pl.DeviceIdType.MESH
F32 = jnp.float32
BF16 = jnp.bfloat16
SCALE = 192.0 ** (-0.5)
SEMS = 112


def iota(shape, axis):
    return lax.broadcasted_iota(jnp.int32, shape, axis)


def by(value, n):
    return ((value.astype(F32) + 0.5) * (1.0 / n)).astype(jnp.int32)


def dot(a, b):
    return jnp.dot(a, b, preferred_element_type=F32)


def dot_t(a, b):
    return lax.dot_general(a, b, (((1,), (1,)), ((), ())), preferred_element_type=F32)


def one_hot(hit):
    return jnp.where(hit, 1.0, 0.0).astype(BF16)


def kernel(
    q_hbm, cache_hbm, len_hbm, slot_hbm, wuv_hbm, wo_hbm, resid_hbm, gain_hbm, wg_hbm, wu_hbm, wd_hbm,
    out_ref,
    len_ref, slot_ref, gain_ref,
    q_v, cache_v, wuv_v, resid_v, w_raw, wd_v,
    lat_s, msg_s, abuf, perm_s, z_s, wo_raw, wo_s, r_s, p_s, b_rx,
    hid, w_s, ss_s, ss_rx, gu_s, d_rx, act_s,
    pt_s, rows_s, pad_s, t_s, hm_s, hm_rx, hid_out,
    e1_s, e1_rx, e2_s, e2_rx, u_s, e3_s, e3_rx,
    sems,
):
    dp, t = lax.axis_index("dp"), lax.axis_index("tp")
    c = lax.rem(dp, 2)
    zh = lax.rem(dp // 2, 2)
    y = lax.rem(dp // 4, 4)
    x = dp // 16
    place = dp // 2
    sib = 1 - c
    other = 1 - zh

    def dev(x_, y_, zh_, c_, t_):
        return (((x_ * 4 + y_) * 2 + zh_) * 2 + c_, t_)

    def turn(v, k):
        return lax.rem(v + k + 4, 4)

    used = [0]

    def sem():
        used[0] += 1
        return sems.at[used[0] - 1]

    sends, tails = [], []

    def finish():
        for tail in tails:
            tail()
        for cp in sends:
            cp.wait()

    def remote(src, dst, ss, rs, to):
        return pltpu.make_async_remote_copy(
            src_ref=src, dst_ref=dst, send_sem=ss, recv_sem=rs, device_id=to, device_id_type=MESH
        )

    def group(copies, whole):
        ss, rs = sem(), sem()
        for src, dst, to in copies:
            remote(src, dst, ss, rs, to).start()
        sends.append(pltpu.make_async_copy(whole, whole, ss))
        return landing(whole, rs)

    def landing(whole, rs):
        return pltpu.make_async_copy(whole, whole, rs)

    def send(src, dst, to, lands):
        return group([(src, dst, to)], lands)

    def load(src, dst):
        cp = pltpu.make_async_copy(src, dst, sem())
        cp.start()
        return cp

    sib_dev = dev(x, y, zh, sib, t)
    zh_dev = dev(x, y, other, c, t)
    x_dev = [dev(turn(x, k), y, zh, c, t) for k in range(4)]
    y_dev = [dev(x, turn(y, k), zh, c, t) for k in range(4)]
    t_dev = [(dp, turn(t, k)) for k in range(4)]

    len_in = load(len_hbm, len_ref)
    q_in = load(q_hbm, q_v)
    cache_in = load(cache_hbm, cache_v)
    wuv_in = [load(wuv_hbm.at[pl.ds(16 * i, 16)], wuv_v.at[pl.ds(16 * i, 16)]) for i in range(2)]
    barrier = pltpu.get_barrier_semaphore()
    for d in [sib_dev, zh_dev] + x_dev[1:] + y_dev[1:] + t_dev[1:]:
        pl.semaphore_signal(barrier, inc=1, device_id=d, device_id_type=MESH)
    for k in range(8):

        @pl.when(jnp.logical_or(x != t, zh * 4 + t != k))
        def _():
            pl.semaphore_signal(
                barrier, inc=1, device_id=dev(t, y, k // 4, c, k % 4), device_id_type=MESH
            )

    for j in range(4):
        lat_s[j, pl.ds(6, 32, 8), :] = jnp.zeros((32, 128), F32)
        lat_s[j, pl.ds(7, 32, 8), :] = jnp.zeros((32, 128), F32)
    len_in.wait()
    q_in.wait()
    cache_in.wait()
    later = [
        load(slot_hbm, slot_ref),
        load(gain_hbm, gain_ref),
        load(resid_hbm, resid_v.at[c]),
        load(wo_hbm, wo_raw.at[pl.ds(pl.multiple_of(128 * c, 128), 112)]),
        load(wg_hbm, w_raw.at[0, c]),
        load(wu_hbm, w_raw.at[1, c]),
        load(wd_hbm.at[pl.ds(0, 256)], wd_v.at[pl.ds(pl.multiple_of(256 * c, 256), 256)]),
        load(wd_hbm.at[pl.ds(256, 32)], wd_v.at[pl.ds(pl.multiple_of(512 + 32 * c, 32), 32)]),
    ]
    scores = []
    for r in range(6):
        live = iota((32, 320), 1) < len_ref[r]
        scores.append(jnp.where(live, dot_t(q_v[r], cache_v[r]) * SCALE, -1e30))
    scores = jnp.concatenate(scores, axis=0)
    weights = jnp.exp(scores - jnp.max(scores, axis=1, keepdims=True))
    probs = (weights * (1.0 / jnp.sum(weights, axis=1, keepdims=True))).astype(BF16)
    for r in range(6):
        latent = dot(probs[32 * r : 32 * r + 32], cache_v[r, :, :512])
        for j in range(4):
            lat_s[j, pl.ds(r, 32, 8), :] = latent[:, 128 * j : 128 * j + 128]
    for half in range(2):
        wuv_in[half].wait()
        for low in range(8):
            for high in range(2):
                h = half * 16 + low * 2 + high
                latent = [lat_s[j, 8 * h : 8 * h + 8, :].astype(BF16) for j in range(4)]
                value = dot(jnp.concatenate(latent, axis=1), wuv_v[h])
                for i in range(3):
                    msg_s[i, half, 2 * low : 2 * low + 2, 128 * high : 128 * high + 128] = value[2 * i : 2 * i + 2]
    for i in range(3):
        for half in range(2):
            abuf[i, half, zh, x, y] = msg_s[i, half].astype(BF16)

    pl.semaphore_wait(barrier, 19 - jnp.where(x == t, 1, 0))

    every = slice(None)

    def first(block, whole):
        out = []
        for k in range(1, 4):
            out.append((block(0, x, y), block(0, x, y), x_dev[k]))
            out.append((block(1, x, y), block(1, x, y), y_dev[k]))
        return group(out, whole)

    def second(block, whole):
        out = []
        for k in range(1, 4):
            out.append((block(0, every, y), block(0, every, y), y_dev[k]))
            out.append((block(1, x, every), block(1, x, every), x_dev[k]))
        return group(out, whole)

    def values_at(i, z_):
        def block(half, x_, y_):
            return abuf.at[i, half, z_, x_, y_]

        return block

    def near_second(i):
        near_in[i].wait()
        near_in[i] = second(values_at(i, zh), abuf.at[i, 0:2, 0, 0:3])

    def far_first(i):
        far_in[i].wait()
        far_in[i] = first(values_at(i, other), abuf.at[i, 0, 0, 0:3, 0:2])

    def far_second(i):
        far_in[i].wait()
        far_in[i] = second(values_at(i, other), abuf.at[i, 0:2, 0, 0:3])

    near_in, far_in = [], []
    for i in range(3):
        mine = abuf.at[i, :, zh, x, y]
        far_in.append(send(mine, mine, zh_dev, abuf.at[i, :, other, x, y]))
        near_in.append(first(values_at(i, zh), abuf.at[i, 0, 0, 0:3, 0:2]))
    for cp in later:
        cp.wait()
    theirs = [
        send(resid_v.at[c], resid_v.at[c], sib_dev, resid_v.at[sib]),
        send(w_raw.at[:, c], w_raw.at[:, c], sib_dev, w_raw.at[:, sib]),
    ]
    for ref, at, step_, n in ((wo_raw, 0, 128, 112), (wd_v, 0, 256, 256), (wd_v, 512, 32, 32)):
        ours = ref.at[pl.ds(pl.multiple_of(at + step_ * c, step_), n)]
        other_half = ref.at[pl.ds(pl.multiple_of(at + step_ * sib, step_), n)]
        theirs.append(send(ours, ours, sib_dev, other_half))
    row, col = iota((256, 256), 0), iota((256, 256), 1)
    perm_s[...] = one_hot(col == row % 32 // 2 * 16 + row // 32 * 2 + row % 2)
    near_second(0)
    near_second(1)
    far_first(0)
    far_first(1)
    far_first(2)
    near_second(2)

    def slot_at(core, line):
        chip = line % 32 // 2 * 2 + line % 64 // 32
        return (chip * 2 + core) * 6 + line // 64 * 2 + line % 2

    order_c = one_hot(iota((192, 384), 1) == slot_at(c, iota((192, 384), 0)))
    slots = jnp.broadcast_to(slot_ref[...][None, :], (384, 384))
    moved = dot_t(order_c, one_hot(slots == iota((384, 384), 0))).astype(BF16)
    for cp in theirs:
        cp.wait()
    r_s[...] = jnp.zeros((192, 256), F32)
    for k in range(2):
        r_s[:, 128 * k : 128 * k + 112] = dot_t(moved, resid_v[k])
        wo_raw[128 * k + 112 : 128 * k + 128, :] = jnp.zeros((16, 4096), BF16)
    for k in range(8):
        wo_s[512 * k : 512 * k + 512, :] = wo_raw[:, 512 * k : 512 * k + 512].T
    far_second(0)
    gains = gain_ref[...].astype(F32)[None, :]
    gains = sum(jnp.where(t == k, gains[:, 1792 * k : 1792 * k + 1792], 0.0) for k in range(4))

    def spread(block, part, at):
        block = (block.astype(F32) * gains[:, 896 * part : 896 * part + 896]).astype(BF16).T
        for j in range(8 * part, 8 * part + 8):
            row, src = 128 * (j % 2 * 8 + j // 2), 112 * (j - 8 * part)
            w_s[row : row + 112, at : at + block.shape[1]] = block[src : src + 112]

    def turn_weights(part):
        cols = slice(896 * part, 896 * part + 896)
        for k in range(2):
            for half in range(2):
                spread(w_raw[k, half, 0:256, cols], part, 512 * k + 256 * half)
        rest = [w_raw[k, half, 256:288, cols] for k in range(2) for half in range(2)]
        spread(jnp.concatenate(rest, axis=0), part, 1024)

    for j in range(16):
        w_s[128 * j + 112 : 128 * j + 128, :] = jnp.zeros((16, 1152), BF16)
    turn_weights(0)
    far_second(1)
    turn_weights(1)
    far_second(2)

    def project(i):
        near_in[i].wait()
        far_in[i].wait()
        for z_ in range(2):
            for half in range(2):
                placed = dot(perm_s[...], abuf[i, half, z_].reshape(256, 256)).astype(BF16)
                for low in range(8):
                    at = half * 2048 + low * 256
                    z_s[32 * z_ : 32 * z_ + 32, at : at + 256] = placed[32 * low : 32 * low + 32]
        partial = dot(z_s[...], wo_s[...]) + jnp.where(t == 0, r_s[64 * i : 64 * i + 64], 0.0)
        p_s[4 * i : 4 * i + 4] = partial.astype(BF16).reshape(4, 16, 256)

    b_sent, b_in = sem(), [sem() for _ in range(3)]
    own = x == t

    def deal(i):
        for k in range(4):
            for z_ in range(2):
                src, dst = p_s.at[4 * i + turn(x, k)], b_rx.at[8 * i + 4 * zh + t]
                to = dev(turn(x, k), y, lax.rem(zh + z_, 2), c, x)
                if k + z_ > 0:
                    remote(src, dst, b_sent, b_in[i], to).start()
                else:

                    @pl.when(jnp.logical_not(own))
                    def _():
                        remote(src, dst, b_sent, b_in[i], to).start()

                    @pl.when(own)
                    def _():
                        pltpu.make_async_copy(src, dst, b_in[i]).start()

    def sent():
        for n, when in ((24, jnp.logical_not(own)), (21, own)):

            @pl.when(when)
            def _():
                pltpu.make_async_copy(b_rx.at[0:n], b_rx.at[0:n], b_sent).wait()

    tails.append(sent)
    for i in range(3):
        project(i)
        deal(i)

    line = iota((16, 384), 0)
    want = jnp.where(line % 8 < 6, (place * 2 + line // 8) * 6 + line % 8, -1)
    t_s[...] = dot_t(one_hot(slots[:16] == want), order_c).astype(BF16)
    col = iota((384, 384), 1)
    core = jnp.where(col >= 192, 1, 0)
    order = one_hot(iota((384, 384), 0) == slot_at(core, col - 192 * core))

    def pieces(matrix, half):
        for i in range(3):
            pt_s[half, i] = jnp.concatenate(
                [matrix[:, 192 * core + 64 * i : 192 * core + 64 * i + 64] for core in range(2)], axis=1
            ).astype(BF16)

    line = iota((192, 384), 0)
    chip = by(line, 6)
    line -= 6 * chip
    pieces(dot(one_hot(slots[:192] == 12 * chip + 6 * c + line), order), 0)
    chip = (chip // 2 % 4 * 4 + chip // 8) * 2 + chip % 2
    pieces(dot(one_hot(slots[:192] == 12 * chip + 6 * c + line), order), 1)
    line, row = iota((64, 48), 0), iota((64, 48), 1)
    pad_s[...] = one_hot(jnp.logical_and(line % 8 < 6, row == line // 8 * 6 + line % 8))
    wd_v[576:640, :] = jnp.zeros((64, 1792), BF16)

    def blocks(i):
        def block(half, x_, y_):
            rows = pl.ds(0, 64) if x_ is every else pl.ds(pl.multiple_of(16 * x_, 16), 16)
            if y_ is every:
                return hid.at[i, rows, pl.ds(1024 * half, 1024)]
            return hid.at[i, rows, pl.ds(pl.multiple_of(1024 * half + 256 * y_, 256), 256)]

        return block

    def hidden_first(i):
        landing(b_rx.at[8 * i : 8 * i + 8], b_in[i]).wait()
        rows = pl.ds(pl.multiple_of(16 * x, 16), 16)
        for z_ in range(2):
            at = 8 * i + 4 * z_
            hidden = jnp.sum(b_rx[at : at + 4].astype(F32), axis=0).astype(BF16)
            for half in range(2):
                lanes = pl.ds(pl.multiple_of(1024 * half + 256 * y + 128 * z_, 128), 128)
                hid[i, rows, lanes] = hidden[:, 128 * half : 128 * half + 128]
        step.append(first(blocks(i), hid.at[i, 0:16, 0:1536]))

    def hidden_second(i):
        step[i].wait()
        step[i] = second(blocks(i), hid.at[i, :, 0:1536])

    step = []
    hidden_first(0)
    hidden_first(1)
    hidden_second(0)
    hidden_first(2)
    hidden_second(1)
    hidden_second(2)

    def silu(v):
        return v * jax.nn.sigmoid(v)

    def gate_up(i):
        step[i].wait()
        gu_s[i] = dot(hid[i], w_s[...]).astype(BF16).reshape(4, 16, 1152)
        parts = [(gu_s.at[i, turn(t, k)], d_rx.at[i, k - 1], t_dev[k]) for k in range(1, 4)]
        return [group(parts, d_rx.at[i])]

    def squares_of(i):
        squares = jnp.zeros((64, 128), F32)
        for j in range(16):
            block = hid[i, :, 128 * j : 128 * j + 128].astype(F32)
            squares += block * block
        ss_s[i] = lax.dot_general(
            jnp.ones((8, 128), F32), squares, (((1,), (1,)), ((), ())),
            precision=lax.Precision.HIGHEST, preferred_element_type=F32,
        )
        return group([(ss_s.at[i], ss_rx.at[i, k - 1], t_dev[k]) for k in range(1, 4)], ss_rx.at[i])

    def activate(i, copies):
        for cp in copies:
            cp.wait()
        total = gu_s[i, t].astype(F32)
        squares = ss_s[i]
        for k in range(3):
            total += d_rx[i, k].astype(F32)
            squares += ss_rx[i, k]
        here = iota((16, 64), 1) == 16 * t + iota((16, 64), 0)
        squares = jnp.sum(jnp.where(here, squares[0:1], 0.0), axis=1, keepdims=True)
        total *= lax.rsqrt(squares * (1.0 / 7168) + 1e-06)
        rest = total[:, 1024:1152]
        tail = silu(rest) * pltpu.roll(rest, 64, 1)
        act_s[i, c, t, :, 0:512] = (silu(total[:, 0:512]) * total[:, 512:1024]).astype(BF16)
        act_s[i, c, t, :, 512:640] = jnp.where(iota((16, 128), 1) < 64, tail, 0.0).astype(BF16)
        mine = act_s.at[i, c, t]
        return group([(mine, mine, t_dev[k]) for k in range(1, 4)], act_s.at[i, 0, 0:3])

    def share(i, copies):
        copies.wait()
        return send(act_s.at[i, c], act_s.at[i, c], sib_dev, act_s.at[i, sib])

    spots = (x, y)
    rings = (x_dev, y_dev)

    wide = [gate_up(i) for i in range(3)]
    for i in range(3):
        wide[i].append(squares_of(i))
    thin = [activate(i, wide[i]) for i in range(3)]
    hm_s[...] = dot(t_s[...], hid[...].reshape(192, 2048)).reshape(2, 8, 2048)
    hm_in = send(hm_s.at[sib], hm_rx, sib_dev, hm_rx)
    ends = [share(i, thin[i]) for i in range(3)]

    def place(half, i):
        return dot(pt_s[half, i], act_s[i].reshape(128, 640))

    for i in range(2):
        ends[i].wait()
        for half in range(2):
            rows_s[half] = place(half, i) + (rows_s[half] if i else 0.0)
    ends[2].wait()
    cuts = (slice(0, 512), slice(512, 896))
    rows = [(rows_s[half] + place(half, 2)).astype(BF16) for half in range(2)]
    step = []
    for cut in cuts:
        for half in range(2):
            part = dot(rows[half], wd_v[:, 896 * half + cut.start : 896 * half + cut.stop])
            e1_s[half, :, :, cut] = part.astype(BF16).reshape(4, 48, cut.stop - cut.start)
            parts = [
                (e1_s.at[half, turn(spots[half], k), :, cut], e1_rx.at[half, k - 1, :, cut], rings[half][k])
                for k in range(1, 4)
            ]
            step.append(group(parts, e1_rx.at[half, :, :, cut]))
    hm_in.wait()
    state = hm_s[c] + hm_rx[...]
    for j in range(16):
        at = 128 * (j % 2 * 8 + j // 2)
        hid_out[:, 112 * j : 112 * j + 112] = state[:, at : at + 112]
    second_step = []
    for q, cut in enumerate(cuts):
        parts = []
        for half in range(2):
            step[2 * q + half].wait()
            total = e1_s[half, spots[half], :, cut].astype(F32)
            for k in range(3):
                total += e1_rx[half, k, :, cut].astype(F32)
            padded = dot(pad_s[...], total.astype(BF16)).astype(BF16)
            e2_s[half, :, :, cut] = padded.reshape(4, 16, cut.stop - cut.start)
            for k in range(1, 4):
                src = e2_s.at[half, turn(spots[1 - half], k), :, cut]
                parts.append((src, e2_rx.at[half, k - 1, :, cut], rings[1 - half][k]))
        second_step.append(group(parts, e2_rx.at[:, :, :, cut]))
    step = []
    for q, cut in enumerate(cuts):
        second_step[q].wait()
        for half in range(2):
            total = e2_s[half, spots[1 - half], :, cut].astype(F32)
            for k in range(3):
                total += e2_rx[half, k, :, cut].astype(F32)
            u_s[half, :, :, cut] = total.reshape(2, 8, cut.stop - cut.start)
        e3_s[:, cut] = jnp.concatenate([u_s[0, other, :, cut], u_s[1, other, :, cut]], axis=0).astype(BF16)
        step.append(send(e3_s.at[:, cut], e3_rx.at[:, cut], zh_dev, e3_rx.at[:, cut]))
    for q, cut in enumerate(cuts):
        step[q].wait()
        last = e3_rx[:, cut].astype(F32)
        for half in range(2):
            lanes = slice(896 * half + cut.start, 896 * half + cut.stop)
            total = u_s[half, zh, :, cut] + last[8 * half : 8 * half + 8] + hid_out[:, lanes]
            out_ref[:, lanes] = total[0:6].astype(BF16)
    finish()


def on_device(
    queries, latent_cache, lengths, slot_row, w_uv, w_o, resid, norm_gain, w_gate, w_up, w_down
):
    hbm = pl.BlockSpec(memory_space=pl.ANY)
    vmem = pl.BlockSpec(memory_space=pltpu.VMEM)
    scratch = [
        ((384,), jnp.int32),
        ((7168,), BF16),
        ((6, 32, 576), BF16),
        ((6, 320, 576), BF16),
        ((32, 512, 128), BF16),
        ((2, 112, 384), BF16),
        ((2, 2, 288, 1792), BF16),
        ((640, 1792), BF16),
        ((4, 256, 128), F32),
        ((3, 2, 16, 256), F32),
        ((3, 2, 2, 4, 4, 16, 256), BF16),
        ((256, 256), BF16),
        ((64, 4096), BF16),
        ((256, 4096), BF16),
        ((4096, 256), BF16),
        ((192, 256), F32),
        ((12, 16, 256), BF16),
        ((24, 16, 256), BF16),
        ((3, 64, 2048), BF16),
        ((2048, 1152), BF16),
        ((3, 8, 64), F32),
        ((3, 3, 8, 64), F32),
        ((3, 4, 16, 1152), BF16),
        ((3, 3, 16, 1152), BF16),
        ((3, 2, 4, 16, 640), BF16),
        ((2, 3, 192, 128), BF16),
        ((2, 192, 640), F32),
        ((64, 48), BF16),
        ((16, 192), BF16),
        ((2, 8, 2048), F32),
        ((8, 2048), F32),
        ((8, 1792), F32),
        ((2, 4, 48, 896), BF16),
        ((2, 3, 48, 896), BF16),
        ((2, 4, 16, 896), BF16),
        ((2, 3, 16, 896), BF16),
        ((2, 2, 8, 896), F32),
        ((16, 896), BF16),
        ((16, 896), BF16),
    ]
    return pl.pallas_call(
        kernel,
        out_shape=jax.ShapeDtypeStruct((6, 1792), BF16),
        in_specs=[hbm] * 11,
        out_specs=vmem,
        scratch_shapes=[pltpu.SMEM((6,), jnp.int32)]
        + [pltpu.VMEM(s, d) for s, d in scratch]
        + [pltpu.SemaphoreType.DMA((SEMS,))],
        compiler_params=pltpu.CompilerParams(
            collective_id=0, has_side_effects=True, vmem_limit_bytes=58 * 1024 * 1024
        ),
        name="layer",
    )(
        queries, latent_cache, lengths, slot_row, w_uv, w_o.T, resid.T, norm_gain, w_gate.T, w_up.T, w_down
    )


def solution(mesh):
    placed = (
        P("dp", "tp", None),
        P("dp", None, None),
        P("dp"),
        P(),
        P("tp", None, None),
        P("tp", "dp"),
        P(None, "dp"),
        P(),
        P("tp", "dp"),
        P("tp", "dp"),
        P("dp", "tp"),
    )
    return jax.shard_map(
        on_device, mesh=mesh, in_specs=placed, out_specs=P("dp", "tp"), check_vma=False
    )
```

```python
import jax
import jax.numpy as jnp
from jax import lax
from jax.experimental import pallas as pl
from jax.experimental.pallas import tpu as pltpu
from jax.sharding import PartitionSpec as P

MESH = pl.DeviceIdType.MESH
F32 = jnp.float32
BF16 = jnp.bfloat16
SCALE = 192.0 ** (-0.5)
SEMS = 112


def iota(shape, axis):
    return lax.broadcasted_iota(jnp.int32, shape, axis)


def by(value, n):
    return ((value.astype(F32) + 0.5) * (1.0 / n)).astype(jnp.int32)


def dot(a, b):
    return jnp.dot(a, b, preferred_element_type=F32)


def dot_t(a, b):
    return lax.dot_general(a, b, (((1,), (1,)), ((), ())), preferred_element_type=F32)


def one_hot(hit):
    return jnp.where(hit, 1.0, 0.0).astype(BF16)


def kernel(
    q_hbm, cache_hbm, len_hbm, slot_hbm, wuv_hbm, wo_hbm, resid_hbm, gain_hbm, wg_hbm, wu_hbm, wd_hbm,
    out_ref,
    len_ref, slot_ref, gain_ref,
    q_v, cache_v, wuv_v, resid_v, w_raw, wd_v,
    lat_s, msg_s, abuf, perm_s, z_s, wo_raw, wo_s, r_s, p_s, b_rx,
    hid, w_s, ss_s, ss_rx, gu_s, d_rx, act_s,
    pt_s, rows_s, pad_s, t_s, hm_s, hm_rx, hid_out,
    e1_s, e1_rx, e2_s, e2_rx, u_s, e3_s, e3_rx,
    sems,
):
    dp, t = lax.axis_index("dp"), lax.axis_index("tp")
    c = lax.rem(dp, 2)
    zh = lax.rem(dp // 2, 2)
    y = lax.rem(dp // 4, 4)
    x = dp // 16
    place = dp // 2
    sib = 1 - c
    other = 1 - zh

    def dev(x_, y_, zh_, c_, t_):
        return (((x_ * 4 + y_) * 2 + zh_) * 2 + c_, t_)

    def turn(v, k):
        return lax.rem(v + k + 4, 4)

    used = [0]

    def sem():
        used[0] += 1
        return sems.at[used[0] - 1]

    sends, tails = [], []

    def finish():
        for tail in tails:
            tail()
        for cp in sends:
            cp.wait()

    def remote(src, dst, ss, rs, to):
        return pltpu.make_async_remote_copy(
            src_ref=src, dst_ref=dst, send_sem=ss, recv_sem=rs, device_id=to, device_id_type=MESH
        )

    def group(copies, whole):
        ss, rs = sem(), sem()
        for src, dst, to in copies:
            remote(src, dst, ss, rs, to).start()
        sends.append(pltpu.make_async_copy(whole, whole, ss))
        return landing(whole, rs)

    def landing(whole, rs):
        return pltpu.make_async_copy(whole, whole, rs)

    def send(src, dst, to, lands):
        return group([(src, dst, to)], lands)

    def load(src, dst):
        cp = pltpu.make_async_copy(src, dst, sem())
        cp.start()
        return cp

    sib_dev = dev(x, y, zh, sib, t)
    zh_dev = dev(x, y, other, c, t)
    x_dev = [dev(turn(x, k), y, zh, c, t) for k in range(4)]
    y_dev = [dev(x, turn(y, k), zh, c, t) for k in range(4)]
    t_dev = [(dp, turn(t, k)) for k in range(4)]
    apart = (0, 1, 2, 1)
    steps = sorted(
        [(a, b) for a in range(4) for b in range(4) if a + b > 0], key=lambda s: -apart[s[0]] - apart[s[1]]
    )
    plane_dev = [dev(turn(x, a), turn(y, b), zh, c, t) for a, b in steps]
    far_to_near = (
        jnp.where(t == 0, 3, jnp.where(t == 3, 1, 2)),
        jnp.where(t == 1, 3, jnp.where(t == 2, 1, 2)),
        jnp.where(t < 2, 1, 3),
    )

    len_in = load(len_hbm, len_ref)
    q_in = load(q_hbm, q_v)
    cache_in = load(cache_hbm, cache_v)
    wuv_in = [load(wuv_hbm.at[pl.ds(16 * i, 16)], wuv_v.at[pl.ds(16 * i, 16)]) for i in range(2)]
    barrier = pltpu.get_barrier_semaphore()
    for d in [sib_dev, zh_dev] + plane_dev + t_dev[1:]:
        pl.semaphore_signal(barrier, inc=1, device_id=d, device_id_type=MESH)
    for k in range(8):

        @pl.when(jnp.logical_or(x != t, zh * 4 + t != k))
        def _():
            pl.semaphore_signal(
                barrier, inc=1, device_id=dev(t, y, k // 4, c, k % 4), device_id_type=MESH
            )

    for j in range(4):
        lat_s[j, pl.ds(6, 32, 8), :] = jnp.zeros((32, 128), F32)
        lat_s[j, pl.ds(7, 32, 8), :] = jnp.zeros((32, 128), F32)
    len_in.wait()
    q_in.wait()
    cache_in.wait()
    later = [
        load(slot_hbm, slot_ref),
        load(gain_hbm, gain_ref),
        load(resid_hbm, resid_v.at[c]),
        load(wo_hbm, wo_raw.at[pl.ds(pl.multiple_of(128 * c, 128), 112)]),
        load(wg_hbm, w_raw.at[0, c]),
        load(wu_hbm, w_raw.at[1, c]),
        load(wd_hbm.at[pl.ds(0, 256)], wd_v.at[pl.ds(pl.multiple_of(256 * c, 256), 256)]),
        load(wd_hbm.at[pl.ds(256, 32)], wd_v.at[pl.ds(pl.multiple_of(512 + 32 * c, 32), 32)]),
    ]
    scores = []
    for r in range(6):
        live = iota((32, 320), 1) < len_ref[r]
        scores.append(jnp.where(live, dot_t(q_v[r], cache_v[r]) * SCALE, -1e30))
    scores = jnp.concatenate(scores, axis=0)
    weights = jnp.exp(scores - jnp.max(scores, axis=1, keepdims=True))
    probs = (weights * (1.0 / jnp.sum(weights, axis=1, keepdims=True))).astype(BF16)
    for r in range(6):
        latent = dot(probs[32 * r : 32 * r + 32], cache_v[r, :, :512])
        for j in range(4):
            lat_s[j, pl.ds(r, 32, 8), :] = latent[:, 128 * j : 128 * j + 128]
    for half in range(2):
        wuv_in[half].wait()
        for low in range(8):
            for high in range(2):
                h = half * 16 + low * 2 + high
                latent = [lat_s[j, 8 * h : 8 * h + 8, :].astype(BF16) for j in range(4)]
                value = dot(jnp.concatenate(latent, axis=1), wuv_v[h])
                for i in range(3):
                    msg_s[i, half, 2 * low : 2 * low + 2, 128 * high : 128 * high + 128] = value[2 * i : 2 * i + 2]
    for i in range(3):
        for half in range(2):
            abuf[i, half, zh, x, y] = msg_s[i, half].astype(BF16)

    pl.semaphore_wait(barrier, 28 - jnp.where(x == t, 1, 0))

    every = slice(None)

    def first(block, whole):
        out = []
        for k in (2, 1, 3):
            out.append((block(0, x, y), block(0, x, y), x_dev[k]))
            out.append((block(1, x, y), block(1, x, y), y_dev[k]))
        return group(out, whole)

    def second(block, whole):
        out = []
        for k in (2, 1, 3):
            out.append((block(0, every, y), block(0, every, y), y_dev[k]))
            out.append((block(1, x, every), block(1, x, every), x_dev[k]))
        return group(out, whole)

    def values_at(i, z_):
        def block(half, x_, y_):
            return abuf.at[i, half, z_, x_, y_]

        return block

    def near_second(i):
        near_in[i].wait()
        near_in[i] = second(values_at(i, zh), abuf.at[i, 0:2, 0, 0:3])

    def far_first(i):
        far_in[i].wait()
        far_in[i] = first(values_at(i, other), abuf.at[i, 0, 0, 0:3, 0:2])

    def far_second(i):
        far_in[i].wait()
        far_in[i] = second(values_at(i, other), abuf.at[i, 0:2, 0, 0:3])

    near_in, far_in = [], []
    for i in range(3):
        mine = abuf.at[i, :, zh, x, y]
        far_in.append(send(mine, mine, zh_dev, abuf.at[i, :, other, x, y]))
        near_in.append(first(values_at(i, zh), abuf.at[i, 0, 0, 0:3, 0:2]))
    for cp in later:
        cp.wait()
    def trade(ref, at, step_, n):
        ours = ref.at[pl.ds(pl.multiple_of(at + step_ * c, step_), n)]
        yours = ref.at[pl.ds(pl.multiple_of(at + step_ * sib, step_), n)]
        return send(ours, ours, sib_dev, yours)

    theirs = [send(resid_v.at[c], resid_v.at[c], sib_dev, resid_v.at[sib]), trade(wo_raw, 0, 128, 112)]
    weights_in = [
        send(w_raw.at[:, c], w_raw.at[:, c], sib_dev, w_raw.at[:, sib]),
        trade(wd_v, 0, 256, 256),
        trade(wd_v, 512, 32, 32),
    ]
    row, col = iota((256, 256), 0), iota((256, 256), 1)
    perm_s[...] = one_hot(col == row % 32 // 2 * 16 + row // 32 * 2 + row % 2)
    near_second(0)
    near_second(1)
    far_first(0)
    far_first(1)
    far_first(2)
    near_second(2)

    def slot_at(core, line):
        chip = line % 32 // 2 * 2 + line % 64 // 32
        return (chip * 2 + core) * 6 + line // 64 * 2 + line % 2

    order_c = one_hot(iota((192, 384), 1) == slot_at(c, iota((192, 384), 0)))
    slots = jnp.broadcast_to(slot_ref[...][None, :], (384, 384))
    moved = dot_t(order_c, one_hot(slots == iota((384, 384), 0))).astype(BF16)
    for cp in theirs:
        cp.wait()
    r_s[...] = jnp.zeros((192, 256), F32)
    for k in range(2):
        r_s[:, 128 * k : 128 * k + 112] = dot_t(moved, resid_v[k])
        wo_raw[128 * k + 112 : 128 * k + 128, :] = jnp.zeros((16, 4096), BF16)
    for k in range(8):
        wo_s[512 * k : 512 * k + 512, :] = wo_raw[:, 512 * k : 512 * k + 512].T
    for i in range(3):
        far_second(i)

    def project(i):
        near_in[i].wait()
        far_in[i].wait()
        for z_ in range(2):
            for half in range(2):
                placed = dot(perm_s[...], abuf[i, half, z_].reshape(256, 256)).astype(BF16)
                for low in range(8):
                    at = half * 2048 + low * 256
                    z_s[32 * z_ : 32 * z_ + 32, at : at + 256] = placed[32 * low : 32 * low + 32]
        partial = dot(z_s[...], wo_s[...]) + jnp.where(t == 0, r_s[64 * i : 64 * i + 64], 0.0)
        p_s[4 * i : 4 * i + 4] = partial.astype(BF16).reshape(4, 16, 256)

    b_sent, b_in = sem(), [sem() for _ in range(3)]
    own = x == t

    def deal(i):
        for z_ in (1, 0):
            for k in (2, 1, 3, 0):
                src, dst = p_s.at[4 * i + turn(x, k)], b_rx.at[8 * i + 4 * zh + t]
                to = dev(turn(x, k), y, lax.rem(zh + z_, 2), c, x)
                if k + z_ > 0:
                    remote(src, dst, b_sent, b_in[i], to).start()
                else:

                    @pl.when(jnp.logical_not(own))
                    def _():
                        remote(src, dst, b_sent, b_in[i], to).start()

                    @pl.when(own)
                    def _():
                        pltpu.make_async_copy(src, dst, b_in[i]).start()

    def sent():
        for n, when in ((24, jnp.logical_not(own)), (21, own)):

            @pl.when(when)
            def _():
                pltpu.make_async_copy(b_rx.at[0:n], b_rx.at[0:n], b_sent).wait()

    tails.append(sent)
    for i in range(3):
        project(i)
        deal(i)


    for cp in weights_in:
        cp.wait()
    gains = gain_ref[...].astype(F32)[None, :]
    gains = sum(jnp.where(t == k, gains[:, 1792 * k : 1792 * k + 1792], 0.0) for k in range(4))

    def spread(block, part, at):
        block = (block.astype(F32) * gains[:, 896 * part : 896 * part + 896]).astype(BF16).T
        for j in range(8 * part, 8 * part + 8):
            row, src = 128 * (j // 4 * 4 + j % 2 * 2 + j // 2 % 2), 112 * (j - 8 * part)
            w_s[row : row + 112, at : at + block.shape[1]] = block[src : src + 112]

    def turn_weights(part):
        cols = slice(896 * part, 896 * part + 896)
        for k in range(2):
            for half in range(2):
                spread(w_raw[k, half, 0:256, cols], part, 512 * k + 256 * half)
        rest = [w_raw[k, half, 256:288, cols] for k in range(2) for half in range(2)]
        spread(jnp.concatenate(rest, axis=0), part, 1024)

    for j in range(16):
        w_s[128 * j + 112 : 128 * j + 128, :] = jnp.zeros((16, 1152), BF16)
    turn_weights(0)
    turn_weights(1)

    def hidden_first(i):
        landing(b_rx.at[8 * i : 8 * i + 8], b_in[i]).wait()
        rows = pl.ds(pl.multiple_of(16 * x, 16), 16)
        for z_ in range(2):
            at = 8 * i + 4 * z_
            hidden = jnp.sum(b_rx[at : at + 4].astype(F32), axis=0).astype(BF16)
            for half in range(2):
                lanes = pl.ds(pl.multiple_of(512 * y + 256 * half + 128 * z_, 128), 128)
                hid[i, rows, lanes] = hidden[:, 128 * half : 128 * half + 128]
        mine = hid.at[i, rows, pl.ds(pl.multiple_of(512 * y, 512), 512)]
        step.append(group([(mine, mine, d) for d in plane_dev], z_s.at[0:48, 0:2560]))

    step = []
    for i in range(3):
        hidden_first(i)

    def silu(v):
        return v * jax.nn.sigmoid(v)

    def gate_up(i):
        step[i].wait()
        gu_s[i] = dot(hid[i], w_s[...]).astype(BF16).reshape(4, 16, 1152)
        parts = [(gu_s.at[i, turn(t, k)], d_rx.at[i, k - 1], (dp, turn(t, k))) for k in far_to_near]
        return [group(parts, d_rx.at[i])]

    def squares_of(i):
        squares = jnp.zeros((64, 128), F32)
        for j in range(16):
            block = hid[i, :, 128 * j : 128 * j + 128].astype(F32)
            squares += block * block
        ss_s[i] = lax.dot_general(
            jnp.ones((8, 128), F32), squares, (((1,), (1,)), ((), ())),
            precision=lax.Precision.HIGHEST, preferred_element_type=F32,
        )
        return group([(ss_s.at[i], ss_rx.at[i, k - 1], t_dev[k]) for k in range(1, 4)], ss_rx.at[i])

    def activate(i, copies):
        for cp in copies:
            cp.wait()
        total = gu_s[i, t].astype(F32)
        squares = ss_s[i]
        for k in range(3):
            total += d_rx[i, k].astype(F32)
            squares += ss_rx[i, k]
        here = iota((16, 64), 1) == 16 * t + iota((16, 64), 0)
        squares = jnp.sum(jnp.where(here, squares[0:1], 0.0), axis=1, keepdims=True)
        total *= lax.rsqrt(squares * (1.0 / 7168) + 1e-06)
        rest = total[:, 1024:1152]
        tail = silu(rest) * pltpu.roll(rest, 64, 1)
        act_s[i, c, t, :, 0:512] = (silu(total[:, 0:512]) * total[:, 512:1024]).astype(BF16)
        act_s[i, c, t, :, 512:640] = jnp.where(iota((16, 128), 1) < 64, tail, 0.0).astype(BF16)
        mine = act_s.at[i, c, t]
        return group([(mine, mine, (dp, turn(t, k))) for k in far_to_near], act_s.at[i, 0, 0:3])

    def share(i, copies):
        copies.wait()
        return send(act_s.at[i, c], act_s.at[i, c], sib_dev, act_s.at[i, sib])

    spots = (x, y)
    rings = (x_dev, y_dev)

    wide = [gate_up(i) for i in range(3)]
    for i in range(3):
        wide[i].append(squares_of(i))
    line = iota((16, 384), 0)
    want = jnp.where(line % 8 < 6, (place * 2 + line // 8) * 6 + line % 8, -1)
    t_s[...] = dot_t(one_hot(slots[:16] == want), order_c).astype(BF16)
    col = iota((384, 384), 1)
    core = jnp.where(col >= 192, 1, 0)
    order = one_hot(iota((384, 384), 0) == slot_at(core, col - 192 * core))

    def pieces(matrix, half):
        for i in range(3):
            pt_s[half, i] = jnp.concatenate(
                [matrix[:, 192 * core + 64 * i : 192 * core + 64 * i + 64] for core in range(2)], axis=1
            ).astype(BF16)

    line = iota((192, 384), 0)
    chip = by(line, 6)
    line -= 6 * chip
    pieces(dot(one_hot(slots[:192] == 12 * chip + 6 * c + line), order), 0)
    chip = (chip // 2 % 4 * 4 + chip // 8) * 2 + chip % 2
    pieces(dot(one_hot(slots[:192] == 12 * chip + 6 * c + line), order), 1)
    line, row = iota((64, 48), 0), iota((64, 48), 1)
    pad_s[...] = one_hot(jnp.logical_and(line % 8 < 6, row == line // 8 * 6 + line % 8))
    wd_v[576:640, :] = jnp.zeros((64, 1792), BF16)
    thin = [activate(i, wide[i]) for i in range(3)]
    hm_s[...] = dot(t_s[...], hid[...].reshape(192, 2048)).reshape(2, 8, 2048)
    hm_in = send(hm_s.at[sib], hm_rx, sib_dev, hm_rx)
    ends = [share(i, thin[i]) for i in range(3)]

    def place(half, i):
        return dot(pt_s[half, i], act_s[i].reshape(128, 640))

    for i in range(2):
        ends[i].wait()
        for half in range(2):
            rows_s[half] = place(half, i) + (rows_s[half] if i else 0.0)
    ends[2].wait()
    cuts = (slice(0, 512), slice(512, 896))
    rows = [(rows_s[half] + place(half, 2)).astype(BF16) for half in range(2)]
    step = []
    for cut in cuts:
        for half in range(2):
            part = dot(rows[half], wd_v[:, 896 * half + cut.start : 896 * half + cut.stop])
            e1_s[half, :, :, cut] = part.astype(BF16).reshape(4, 48, cut.stop - cut.start)
            parts = [
                (e1_s.at[half, turn(spots[half], k), :, cut], e1_rx.at[half, k - 1, :, cut], rings[half][k])
                for k in (2, 1, 3)
            ]
            step.append(group(parts, e1_rx.at[half, :, :, cut]))
    hm_in.wait()
    state = hm_s[c] + hm_rx[...]
    for j in range(16):
        at = 128 * (j // 4 * 4 + j % 2 * 2 + j // 2 % 2)
        hid_out[:, 112 * j : 112 * j + 112] = state[:, at : at + 112]
    second_step = []
    for q, cut in enumerate(cuts):
        parts = []
        for half in range(2):
            step[2 * q + half].wait()
            total = e1_s[half, spots[half], :, cut].astype(F32)
            for k in range(3):
                total += e1_rx[half, k, :, cut].astype(F32)
            padded = dot(pad_s[...], total.astype(BF16)).astype(BF16)
            e2_s[half, :, :, cut] = padded.reshape(4, 16, cut.stop - cut.start)
            for k in (2, 1, 3):
                src = e2_s.at[half, turn(spots[1 - half], k), :, cut]
                parts.append((src, e2_rx.at[half, k - 1, :, cut], rings[1 - half][k]))
        second_step.append(group(parts, e2_rx.at[:, :, :, cut]))
    step = []
    for q, cut in enumerate(cuts):
        second_step[q].wait()
        for half in range(2):
            total = e2_s[half, spots[1 - half], :, cut].astype(F32)
            for k in range(3):
                total += e2_rx[half, k, :, cut].astype(F32)
            u_s[half, :, :, cut] = total.reshape(2, 8, cut.stop - cut.start)
        e3_s[:, cut] = jnp.concatenate([u_s[0, other, :, cut], u_s[1, other, :, cut]], axis=0).astype(BF16)
        step.append(send(e3_s.at[:, cut], e3_rx.at[:, cut], zh_dev, e3_rx.at[:, cut]))
    for q, cut in enumerate(cuts):
        step[q].wait()
        last = e3_rx[:, cut].astype(F32)
        for half in range(2):
            lanes = slice(896 * half + cut.start, 896 * half + cut.stop)
            total = u_s[half, zh, :, cut] + last[8 * half : 8 * half + 8] + hid_out[:, lanes]
            out_ref[:, lanes] = total[0:6].astype(BF16)
    finish()


def on_device(
    queries, latent_cache, lengths, slot_row, w_uv, w_o, resid, norm_gain, w_gate, w_up, w_down
):
    hbm = pl.BlockSpec(memory_space=pl.ANY)
    vmem = pl.BlockSpec(memory_space=pltpu.VMEM)
    scratch = [
        ((384,), jnp.int32),
        ((7168,), BF16),
        ((6, 32, 576), BF16),
        ((6, 320, 576), BF16),
        ((32, 512, 128), BF16),
        ((2, 112, 384), BF16),
        ((2, 2, 288, 1792), BF16),
        ((640, 1792), BF16),
        ((4, 256, 128), F32),
        ((3, 2, 16, 256), F32),
        ((3, 2, 2, 4, 4, 16, 256), BF16),
        ((256, 256), BF16),
        ((64, 4096), BF16),
        ((256, 4096), BF16),
        ((4096, 256), BF16),
        ((192, 256), F32),
        ((12, 16, 256), BF16),
        ((24, 16, 256), BF16),
        ((3, 64, 2048), BF16),
        ((2048, 1152), BF16),
        ((3, 8, 64), F32),
        ((3, 3, 8, 64), F32),
        ((3, 4, 16, 1152), BF16),
        ((3, 3, 16, 1152), BF16),
        ((3, 2, 4, 16, 640), BF16),
        ((2, 3, 192, 128), BF16),
        ((2, 192, 640), F32),
        ((64, 48), BF16),
        ((16, 192), BF16),
        ((2, 8, 2048), F32),
        ((8, 2048), F32),
        ((8, 1792), F32),
        ((2, 4, 48, 896), BF16),
        ((2, 3, 48, 896), BF16),
        ((2, 4, 16, 896), BF16),
        ((2, 3, 16, 896), BF16),
        ((2, 2, 8, 896), F32),
        ((16, 896), BF16),
        ((16, 896), BF16),
    ]
    return pl.pallas_call(
        kernel,
        out_shape=jax.ShapeDtypeStruct((6, 1792), BF16),
        in_specs=[hbm] * 11,
        out_specs=vmem,
        scratch_shapes=[pltpu.SMEM((6,), jnp.int32)]
        + [pltpu.VMEM(s, d) for s, d in scratch]
        + [pltpu.SemaphoreType.DMA((SEMS,))],
        compiler_params=pltpu.CompilerParams(
            collective_id=0, has_side_effects=True, vmem_limit_bytes=58 * 1024 * 1024
        ),
        name="layer",
    )(
        queries, latent_cache, lengths, slot_row, w_uv, w_o.T, resid.T, norm_gain, w_gate.T, w_up.T, w_down
    )


def solution(mesh):
    placed = (
        P("dp", "tp", None),
        P("dp", None, None),
        P("dp"),
        P(),
        P("tp", None, None),
        P("tp", "dp"),
        P(None, "dp"),
        P(),
        P("tp", "dp"),
        P("tp", "dp"),
        P("dp", "tp"),
    )
    return jax.shard_map(
        on_device, mesh=mesh, in_specs=placed, out_specs=P("dp", "tp"), check_vma=False
    )
```

```python
import jax
import jax.numpy as jnp
from jax import lax
from jax.experimental import pallas as pl
from jax.experimental.pallas import tpu as pltpu
from jax.sharding import PartitionSpec as P

MESH = pl.DeviceIdType.MESH
F32 = jnp.float32
BF16 = jnp.bfloat16
SCALE = 192.0 ** (-0.5)
SEMS = 101


def iota(shape, axis):
    return lax.broadcasted_iota(jnp.int32, shape, axis)


def by(value, n):
    return ((value.astype(F32) + 0.5) * (1.0 / n)).astype(jnp.int32)


def dot(a, b):
    return jnp.dot(a, b, preferred_element_type=F32)


def dot_t(a, b):
    return lax.dot_general(a, b, (((1,), (1,)), ((), ())), preferred_element_type=F32)


def one_hot(hit):
    return jnp.where(hit, 1.0, 0.0).astype(BF16)


def kernel(
    q_hbm, cache_hbm, len_hbm, slot_hbm, wuv_hbm, wo_hbm, resid_hbm, gain_hbm, wg_hbm, wu_hbm, wd_hbm,
    out_ref,
    len_ref, slot_ref, gain_ref,
    q_v, cache_v, wuv_v, resid_v, w_raw, wd_v,
    lat_s, msg_s, abuf, perm_s, z_s, wo_raw, wo_s, r_s, p_s, b_rx,
    hid, w_s, ss_s, ss_rx, gu_s, d_rx, act_s,
    pt_s, rows_s, pad_s, t_s, hm_s, hm_rx, hid_out,
    e1_s, e1_rx, e2_s, e2_rx, u_s, e3_s, e3_rx,
    sems,
):
    dp, t = lax.axis_index("dp"), lax.axis_index("tp")
    c = lax.rem(dp, 2)
    zh = lax.rem(dp // 2, 2)
    y = lax.rem(dp // 4, 4)
    x = dp // 16
    place = dp // 2
    sib = 1 - c
    other = 1 - zh

    def dev(x_, y_, zh_, c_, t_):
        return (((x_ * 4 + y_) * 2 + zh_) * 2 + c_, t_)

    def turn(v, k):
        return lax.rem(v + k + 4, 4)

    used = [0]

    def sem():
        used[0] += 1
        return sems.at[used[0] - 1]

    sends, tails = [], []

    def finish():
        for tail in tails:
            tail()
        for cp in sends:
            cp.wait()

    def remote(src, dst, ss, rs, to):
        return pltpu.make_async_remote_copy(
            src_ref=src, dst_ref=dst, send_sem=ss, recv_sem=rs, device_id=to, device_id_type=MESH
        )

    def group(copies, whole):
        ss, rs = sem(), sem()
        for src, dst, to in copies:
            remote(src, dst, ss, rs, to).start()
        sends.append(pltpu.make_async_copy(whole, whole, ss))
        return landing(whole, rs)

    def landing(whole, rs):
        return pltpu.make_async_copy(whole, whole, rs)

    def send(src, dst, to, lands):
        return group([(src, dst, to)], lands)

    def load(src, dst):
        cp = pltpu.make_async_copy(src, dst, sem())
        cp.start()
        return cp

    sib_dev = dev(x, y, zh, sib, t)
    zh_dev = dev(x, y, other, c, t)
    x_dev = [dev(turn(x, k), y, zh, c, t) for k in range(4)]
    y_dev = [dev(x, turn(y, k), zh, c, t) for k in range(4)]
    t_dev = [(dp, turn(t, k)) for k in range(4)]
    apart = (0, 1, 2, 1)
    steps = sorted(
        [(a, b) for a in range(4) for b in range(4) if a + b > 0], key=lambda s: -apart[s[0]] - apart[s[1]]
    )
    plane_dev = [dev(turn(x, a), turn(y, b), zh, c, t) for a, b in steps]
    far_to_near = (
        jnp.where(t == 0, 3, jnp.where(t == 3, 1, 2)),
        jnp.where(t == 1, 3, jnp.where(t == 2, 1, 2)),
        jnp.where(t < 2, 1, 3),
    )

    len_in = load(len_hbm, len_ref)
    q_in = load(q_hbm, q_v)
    cache_in = load(cache_hbm, cache_v)
    wuv_in = [load(wuv_hbm.at[pl.ds(16 * i, 16)], wuv_v.at[pl.ds(16 * i, 16)]) for i in range(2)]
    barrier = pltpu.get_barrier_semaphore()
    for d in [sib_dev, zh_dev] + plane_dev + t_dev[1:]:
        pl.semaphore_signal(barrier, inc=1, device_id=d, device_id_type=MESH)
    for k in range(8):

        @pl.when(jnp.logical_or(x != t, zh * 4 + t != k))
        def _():
            pl.semaphore_signal(
                barrier, inc=1, device_id=dev(t, y, k // 4, c, k % 4), device_id_type=MESH
            )

    for j in range(4):
        lat_s[j, pl.ds(6, 32, 8), :] = jnp.zeros((32, 128), F32)
        lat_s[j, pl.ds(7, 32, 8), :] = jnp.zeros((32, 128), F32)
    len_in.wait()
    q_in.wait()
    cache_in.wait()
    later = [
        load(slot_hbm, slot_ref),
        load(gain_hbm, gain_ref),
        load(resid_hbm, resid_v.at[c]),
        load(wo_hbm, wo_raw.at[pl.ds(pl.multiple_of(128 * c, 128), 112)]),
        load(wg_hbm, w_raw.at[0, c]),
        load(wu_hbm, w_raw.at[1, c]),
        load(wd_hbm.at[pl.ds(0, 256)], wd_v.at[pl.ds(pl.multiple_of(256 * c, 256), 256)]),
        load(wd_hbm.at[pl.ds(256, 32)], wd_v.at[pl.ds(pl.multiple_of(512 + 32 * c, 32), 32)]),
    ]
    scores = []
    for r in range(6):
        live = iota((32, 320), 1) < len_ref[r]
        scores.append(jnp.where(live, dot_t(q_v[r], cache_v[r]) * SCALE, -1e30))
    scores = jnp.concatenate(scores, axis=0)
    weights = jnp.exp(scores - jnp.max(scores, axis=1, keepdims=True))
    probs = (weights * (1.0 / jnp.sum(weights, axis=1, keepdims=True))).astype(BF16)
    for r in range(6):
        latent = dot(probs[32 * r : 32 * r + 32], cache_v[r, :, :512])
        for j in range(4):
            lat_s[j, pl.ds(r, 32, 8), :] = latent[:, 128 * j : 128 * j + 128]
    for half in range(2):
        wuv_in[half].wait()
        for low in range(8):
            for high in range(2):
                h = half * 16 + low * 2 + high
                latent = [lat_s[j, 8 * h : 8 * h + 8, :].astype(BF16) for j in range(4)]
                value = dot(jnp.concatenate(latent, axis=1), wuv_v[h])
                for i in range(3):
                    msg_s[i, half, 2 * low : 2 * low + 2, 128 * high : 128 * high + 128] = value[2 * i : 2 * i + 2]
    for i in range(3):
        for half in range(2):
            abuf[i, half, zh, x, y] = msg_s[i, half].astype(BF16)

    pl.semaphore_wait(barrier, 28 - jnp.where(x == t, 1, 0))

    every = slice(None)

    def first(block, whole):
        out = []
        for k in (2, 1, 3):
            out.append((block(0, x, y), block(0, x, y), x_dev[k]))
            out.append((block(1, x, y), block(1, x, y), y_dev[k]))
        return group(out, whole)

    def second(block, whole):
        out = []
        for k in (2, 1, 3):
            out.append((block(0, every, y), block(0, every, y), y_dev[k]))
            out.append((block(1, x, every), block(1, x, every), x_dev[k]))
        return group(out, whole)

    def values_at(i, z_):
        def block(half, x_, y_):
            return abuf.at[i, half, z_, x_, y_]

        return block

    def near_second(i):
        near_in[i].wait()
        near_in[i] = second(values_at(i, zh), abuf.at[i, 0:2, 0, 0:3])

    def far_first(i):
        far_in[i].wait()
        far_in[i] = first(values_at(i, other), abuf.at[i, 0, 0, 0:3, 0:2])

    def far_second(i):
        far_in[i].wait()
        far_in[i] = second(values_at(i, other), abuf.at[i, 0:2, 0, 0:3])

    near_in, far_in = [], []
    for i in range(3):
        mine = abuf.at[i, :, zh, x, y]
        far_in.append(send(mine, mine, zh_dev, abuf.at[i, :, other, x, y]))
        near_in.append(first(values_at(i, zh), abuf.at[i, 0, 0, 0:3, 0:2]))
    for cp in later:
        cp.wait()
    def trade(ref, at, step_, n):
        ours = ref.at[pl.ds(pl.multiple_of(at + step_ * c, step_), n)]
        yours = ref.at[pl.ds(pl.multiple_of(at + step_ * sib, step_), n)]
        return send(ours, ours, sib_dev, yours)

    theirs = [send(resid_v.at[c], resid_v.at[c], sib_dev, resid_v.at[sib]), trade(wo_raw, 0, 128, 112)]
    weights_in = [
        send(w_raw.at[:, c], w_raw.at[:, c], sib_dev, w_raw.at[:, sib]),
        trade(wd_v, 0, 256, 256),
        trade(wd_v, 512, 32, 32),
    ]
    row, col = iota((256, 256), 0), iota((256, 256), 1)
    perm_s[...] = one_hot(col == row % 32 // 2 * 16 + row // 32 * 2 + row % 2)
    near_second(0)
    near_second(1)
    far_first(0)
    far_first(1)
    far_first(2)
    near_second(2)

    def slot_at(core, line):
        chip = line % 32 // 2 * 2 + line % 64 // 32
        return (chip * 2 + core) * 6 + line // 64 * 2 + line % 2

    order_c = one_hot(iota((192, 384), 1) == slot_at(c, iota((192, 384), 0)))
    slots = jnp.broadcast_to(slot_ref[...][None, :], (384, 384))
    moved = dot_t(order_c, one_hot(slots == iota((384, 384), 0))).astype(BF16)
    for cp in theirs:
        cp.wait()
    r_s[...] = jnp.zeros((192, 256), F32)
    for k in range(2):
        r_s[:, 128 * k : 128 * k + 112] = dot_t(moved, resid_v[k])
        wo_raw[128 * k + 112 : 128 * k + 128, :] = jnp.zeros((16, 4096), BF16)
    for k in range(8):
        wo_s[512 * k : 512 * k + 512, :] = wo_raw[:, 512 * k : 512 * k + 512].T
    for i in range(3):
        far_second(i)

    def project(i):
        near_in[i].wait()
        far_in[i].wait()
        for z_ in range(2):
            for half in range(2):
                placed = dot(perm_s[...], abuf[i, half, z_].reshape(256, 256)).astype(BF16)
                for low in range(8):
                    at = half * 2048 + low * 256
                    z_s[32 * z_ : 32 * z_ + 32, at : at + 256] = placed[32 * low : 32 * low + 32]
        partial = dot(z_s[...], wo_s[...]) + jnp.where(t == 0, r_s[64 * i : 64 * i + 64], 0.0)
        p_s[4 * i : 4 * i + 4] = partial.astype(BF16).reshape(4, 16, 256)

    b_sent, b_in = sem(), [sem() for _ in range(3)]
    own = x == t

    def deal(i):
        for z_ in (1, 0):
            for k in (2, 1, 3, 0):
                src, dst = p_s.at[4 * i + turn(x, k)], b_rx.at[8 * i + 4 * zh + t]
                to = dev(turn(x, k), y, lax.rem(zh + z_, 2), c, x)
                if k + z_ > 0:
                    remote(src, dst, b_sent, b_in[i], to).start()
                else:

                    @pl.when(jnp.logical_not(own))
                    def _():
                        remote(src, dst, b_sent, b_in[i], to).start()

                    @pl.when(own)
                    def _():
                        pltpu.make_async_copy(src, dst, b_in[i]).start()

    def sent():
        for n, when in ((24, jnp.logical_not(own)), (21, own)):

            @pl.when(when)
            def _():
                pltpu.make_async_copy(b_rx.at[0:n], b_rx.at[0:n], b_sent).wait()

    tails.append(sent)
    for i in range(3):
        project(i)
        deal(i)


    for cp in weights_in:
        cp.wait()
    gains = gain_ref[...].astype(F32)[None, :]
    gains = sum(jnp.where(t == k, gains[:, 1792 * k : 1792 * k + 1792], 0.0) for k in range(4))

    def spread(block, part, at):
        block = (block.astype(F32) * gains[:, 896 * part : 896 * part + 896]).astype(BF16).T
        for j in range(8 * part, 8 * part + 8):
            row, src = 128 * (j // 4 * 4 + j % 2 * 2 + j // 2 % 2), 112 * (j - 8 * part)
            w_s[row : row + 112, at : at + block.shape[1]] = block[src : src + 112]

    def turn_weights(part):
        cols = slice(896 * part, 896 * part + 896)
        for k in range(2):
            for half in range(2):
                spread(w_raw[k, half, 0:256, cols], part, 512 * k + 256 * half)
        rest = [w_raw[k, half, 256:288, cols] for k in range(2) for half in range(2)]
        spread(jnp.concatenate(rest, axis=0), part, 1024)

    for j in range(16):
        w_s[128 * j + 112 : 128 * j + 128, :] = jnp.zeros((16, 1152), BF16)
    turn_weights(0)
    turn_weights(1)

    def hidden_first(i):
        landing(b_rx.at[8 * i : 8 * i + 8], b_in[i]).wait()
        rows = pl.ds(pl.multiple_of(16 * x, 16), 16)
        for z_ in range(2):
            at = 8 * i + 4 * z_
            hidden = jnp.sum(b_rx[at : at + 4].astype(F32), axis=0).astype(BF16)
            for half in range(2):
                lanes = pl.ds(pl.multiple_of(512 * y + 256 * half + 128 * z_, 128), 128)
                hid[i, rows, lanes] = hidden[:, 128 * half : 128 * half + 128]
        mine = hid.at[i, rows, pl.ds(pl.multiple_of(512 * y, 512), 512)]
        step.append(group([(mine, mine, d) for d in plane_dev], z_s.at[0:48, 0:2560]))

    step = []
    for i in range(3):
        hidden_first(i)

    def silu(v):
        return v * jax.nn.sigmoid(v)

    def gate_up(i):
        step[i].wait()
        gu_s[i] = dot(hid[i], w_s[...]).astype(BF16).reshape(4, 16, 1152)
        parts = [(gu_s.at[i, turn(t, k)], d_rx.at[i, k - 1], (dp, turn(t, k))) for k in far_to_near]
        return [group(parts, d_rx.at[i])]

    def squares_of(i):
        squares = jnp.zeros((64, 128), F32)
        for j in range(16):
            block = hid[i, :, 128 * j : 128 * j + 128].astype(F32)
            squares += block * block
        ss_s[i] = lax.dot_general(
            jnp.ones((8, 128), F32), squares, (((1,), (1,)), ((), ())),
            precision=lax.Precision.HIGHEST, preferred_element_type=F32,
        )

    def activate(i, copies):
        for cp in copies:
            cp.wait()
        total = gu_s[i, t].astype(F32)
        squares = ss_s[i]
        for k in range(3):
            total += d_rx[i, k].astype(F32)
            squares += ss_rx[k, i]
        here = iota((16, 64), 1) == 16 * t + iota((16, 64), 0)
        squares = jnp.sum(jnp.where(here, squares[0:1], 0.0), axis=1, keepdims=True)
        total *= lax.rsqrt(squares * (1.0 / 7168) + 1e-06)
        rest = total[:, 1024:1152]
        tail = silu(rest) * pltpu.roll(rest, 64, 1)
        act_s[i, c, t, :, 0:512] = (silu(total[:, 0:512]) * total[:, 512:1024]).astype(BF16)
        act_s[i, c, t, :, 512:640] = jnp.where(iota((16, 128), 1) < 64, tail, 0.0).astype(BF16)
        mine = act_s.at[i, c, t]
        return group([(mine, mine, (dp, turn(t, k))) for k in far_to_near], act_s.at[i, 0, 0:3])

    def share(i, copies):
        copies.wait()
        return send(act_s.at[i, c], act_s.at[i, c], sib_dev, act_s.at[i, sib])

    spots = (x, y)
    rings = (x_dev, y_dev)

    wide = [gate_up(i) for i in range(3)]
    for i in range(3):
        squares_of(i)
    wide[0].append(group([(ss_s, ss_rx.at[k - 1], t_dev[k]) for k in range(1, 4)], ss_rx))
    line = iota((16, 384), 0)
    want = jnp.where(line % 8 < 6, (place * 2 + line // 8) * 6 + line % 8, -1)
    t_s[...] = dot_t(one_hot(slots[:16] == want), order_c).astype(BF16)
    col = iota((384, 384), 1)
    core = jnp.where(col >= 192, 1, 0)
    order = one_hot(iota((384, 384), 0) == slot_at(core, col - 192 * core))

    def pieces(matrix, half):
        for i in range(3):
            pt_s[half, i] = jnp.concatenate(
                [matrix[:, 192 * core + 64 * i : 192 * core + 64 * i + 64] for core in range(2)], axis=1
            ).astype(BF16)

    line = iota((192, 384), 0)
    chip = by(line, 6)
    line -= 6 * chip
    pieces(dot(one_hot(slots[:192] == 12 * chip + 6 * c + line), order), 0)
    chip = (chip // 2 % 4 * 4 + chip // 8) * 2 + chip % 2
    pieces(dot(one_hot(slots[:192] == 12 * chip + 6 * c + line), order), 1)
    line, row = iota((64, 48), 0), iota((64, 48), 1)
    pad_s[...] = one_hot(jnp.logical_and(line % 8 < 6, row == line // 8 * 6 + line % 8))
    wd_v[576:640, :] = jnp.zeros((64, 1792), BF16)
    thin = [activate(i, wide[i]) for i in range(3)]
    hm_s[...] = dot(t_s[...], hid[...].reshape(192, 2048)).reshape(2, 8, 2048)
    hm_in = send(hm_s.at[sib], hm_rx, sib_dev, hm_rx)
    ends = [share(i, thin[i]) for i in range(3)]

    def place(half, i):
        return dot(pt_s[half, i], act_s[i].reshape(128, 640))

    for i in range(2):
        ends[i].wait()
        for half in range(2):
            rows_s[half] = place(half, i) + (rows_s[half] if i else 0.0)
    ends[2].wait()
    cuts = (slice(0, 512), slice(512, 896))
    rows = [(rows_s[half] + place(half, 2)).astype(BF16) for half in range(2)]
    step = []
    for cut in cuts:
        for half in range(2):
            part = dot(rows[half], wd_v[:, 896 * half + cut.start : 896 * half + cut.stop])
            e1_s[half, :, :, cut] = part.astype(BF16).reshape(4, 48, cut.stop - cut.start)
            parts = [
                (e1_s.at[half, turn(spots[half], k), :, cut], e1_rx.at[half, k - 1, :, cut], rings[half][k])
                for k in (2, 1, 3)
            ]
            step.append(group(parts, e1_rx.at[half, :, :, cut]))
    hm_in.wait()
    state = hm_s[c] + hm_rx[...]
    for j in range(16):
        at = 128 * (j // 4 * 4 + j % 2 * 2 + j // 2 % 2)
        hid_out[:, 112 * j : 112 * j + 112] = state[:, at : at + 112]
    second_step = []
    for q, cut in enumerate(cuts):
        parts = []
        for half in range(2):
            step[2 * q + half].wait()
            total = e1_s[half, spots[half], :, cut].astype(F32)
            for k in range(3):
                total += e1_rx[half, k, :, cut].astype(F32)
            padded = dot(pad_s[...], total.astype(BF16)).astype(BF16)
            e2_s[half, :, :, cut] = padded.reshape(4, 16, cut.stop - cut.start)
            for k in (2, 1, 3):
                src = e2_s.at[half, turn(spots[1 - half], k), :, cut]
                parts.append((src, e2_rx.at[half, k - 1, :, cut], rings[1 - half][k]))
        second_step.append(group(parts, e2_rx.at[:, :, :, cut]))
    step = []
    for q, cut in enumerate(cuts):
        second_step[q].wait()
        for half in range(2):
            total = e2_s[half, spots[1 - half], :, cut].astype(F32)
            for k in range(3):
                total += e2_rx[half, k, :, cut].astype(F32)
            u_s[half, :, :, cut] = total.reshape(2, 8, cut.stop - cut.start)
        e3_s[:, cut] = jnp.concatenate([u_s[0, other, :, cut], u_s[1, other, :, cut]], axis=0).astype(BF16)
        step.append(send(e3_s.at[:, cut], e3_rx.at[:, cut], zh_dev, e3_rx.at[:, cut]))
    for q, cut in enumerate(cuts):
        step[q].wait()
        last = e3_rx[:, cut].astype(F32)
        for half in range(2):
            lanes = slice(896 * half + cut.start, 896 * half + cut.stop)
            total = u_s[half, zh, :, cut] + last[8 * half : 8 * half + 8] + hid_out[:, lanes]
            out_ref[:, lanes] = total[0:6].astype(BF16)
    finish()


def on_device(
    queries, latent_cache, lengths, slot_row, w_uv, w_o, resid, norm_gain, w_gate, w_up, w_down
):
    hbm = pl.BlockSpec(memory_space=pl.ANY)
    vmem = pl.BlockSpec(memory_space=pltpu.VMEM)
    scratch = [
        ((384,), jnp.int32),
        ((7168,), BF16),
        ((6, 32, 576), BF16),
        ((6, 320, 576), BF16),
        ((32, 512, 128), BF16),
        ((2, 112, 384), BF16),
        ((2, 2, 288, 1792), BF16),
        ((640, 1792), BF16),
        ((4, 256, 128), F32),
        ((3, 2, 16, 256), F32),
        ((3, 2, 2, 4, 4, 16, 256), BF16),
        ((256, 256), BF16),
        ((64, 4096), BF16),
        ((256, 4096), BF16),
        ((4096, 256), BF16),
        ((192, 256), F32),
        ((12, 16, 256), BF16),
        ((24, 16, 256), BF16),
        ((3, 64, 2048), BF16),
        ((2048, 1152), BF16),
        ((3, 8, 64), F32),
        ((3, 3, 8, 64), F32),
        ((3, 4, 16, 1152), BF16),
        ((3, 3, 16, 1152), BF16),
        ((3, 2, 4, 16, 640), BF16),
        ((2, 3, 192, 128), BF16),
        ((2, 192, 640), F32),
        ((64, 48), BF16),
        ((16, 192), BF16),
        ((2, 8, 2048), F32),
        ((8, 2048), F32),
        ((8, 1792), F32),
        ((2, 4, 48, 896), BF16),
        ((2, 3, 48, 896), BF16),
        ((2, 4, 16, 896), BF16),
        ((2, 3, 16, 896), BF16),
        ((2, 2, 8, 896), F32),
        ((16, 896), BF16),
        ((16, 896), BF16),
    ]
    return pl.pallas_call(
        kernel,
        out_shape=jax.ShapeDtypeStruct((6, 1792), BF16),
        in_specs=[hbm] * 11,
        out_specs=vmem,
        scratch_shapes=[pltpu.SMEM((6,), jnp.int32)]
        + [pltpu.VMEM(s, d) for s, d in scratch]
        + [pltpu.SemaphoreType.DMA((SEMS,))],
        compiler_params=pltpu.CompilerParams(
            collective_id=0, has_side_effects=True, vmem_limit_bytes=58 * 1024 * 1024
        ),
        name="layer",
    )(
        queries, latent_cache, lengths, slot_row, w_uv, w_o.T, resid.T, norm_gain, w_gate.T, w_up.T, w_down
    )


def solution(mesh):
    placed = (
        P("dp", "tp", None),
        P("dp", None, None),
        P("dp"),
        P(),
        P("tp", None, None),
        P("tp", "dp"),
        P(None, "dp"),
        P(),
        P("tp", "dp"),
        P("tp", "dp"),
        P("dp", "tp"),
    )
    return jax.shard_map(
        on_device, mesh=mesh, in_specs=placed, out_specs=P("dp", "tp"), check_vma=False
    )
```
